256 devices in a mesh: seq: 32 (over y, x, core), head: 8 (over z).
Axes of the slice: x: 4, y: 4, z: 8, core: 2. Of those that a mesh axis runs over, the one named last changes fastest.
Arguments:
- tokens: bfloat16 [8192, 2048], P('seq'), may hold values from -60 to 60
- w_query: bfloat16 [2048, 2048], P(None, 'head'), may hold values from -2 to 2
- w_key: bfloat16 [2048, 2048], P(None, 'head'), may hold values from -2 to 2
- w_value: bfloat16 [2048, 2048], P(None, 'head'), may hold values from -0.125 to 0.125
- w_out: bfloat16 [2048, 2048], P('head'), may hold values from -0.125 to 0.125
Outputs:
- mixed: bfloat16 [8192, 2048], P(('seq', 'head'))
The draws below stay inside these ranges and needn't reach their ends.
All inputs are finite; a program needn't handle non-finite values.
Results may differ from the reference program's by a relative error of at most 0.019.
The reference program's roundings to bfloat16 on the way (of `attention`) count: a program that leaves them out, or rounds other values in their place, can miss the bound.
Values may be sent and summed in bfloat16 or wider, within the bound.
A program may use at most 128 MiB of HBM per device.

```python
import math
import jax
import jax.numpy as jnp
from jax import lax

D = 2048
HEADS = 16
HEAD_DIM = 128
LEAF = 128
TOKENS = 8192


def shared_weight(key):
    return jax.random.normal(key, (D, D), jnp.float32) * D ** (-0.5)


def segment_field(key, length, low, high):
    count = (TOKENS + length - 1) // length
    first, second = jax.random.split(key)
    vectors = jax.random.normal(first, (count, D), jnp.float32)
    factors = jnp.exp(jax.random.uniform(second, (count, 1), jnp.float32, low, high))
    owner = jnp.arange(TOKENS) // length
    return (vectors * factors)[owner]


def draw_tokens(key, part):
    key = jax.random.fold_in(key, 13)
    first, second, third = jax.random.split(key, 3)
    base = jnp.clip(jax.random.normal(first, (TOKENS, D), jnp.float32), -6.0, 6.0)
    noise_top = 0.0
    low = 0.0
    high = 0.0
    scales = jnp.exp(jax.random.uniform(second, (TOKENS, 1), jnp.float32, 0.0, noise_top))
    field = base * scales
    lengths = (max(LEAF // 2, 1), 2 * LEAF, 16 * LEAF)
    for index, length in enumerate(lengths):
        field = field + segment_field(jax.random.fold_in(third, index), length, low, high)
    return jnp.clip(field, -60.0, 60.0).astype(jnp.bfloat16)


def draw_w_query(key, part):
    base = shared_weight(key)
    return jnp.clip(base, -1.0, 1.0).astype(jnp.bfloat16)


def draw_w_key(key, part):
    key = jax.random.fold_in(key, 12)
    noise = jax.random.normal(key, (D, D), jnp.float32) * D ** (-0.5)
    return jnp.clip(noise, -1.0, 1.0).astype(jnp.bfloat16)


def level_of(own_key, dims, cuts, least, top_value):
    def one(dim, blocks):
        steps = jax.random.uniform(jax.random.fold_in(jax.random.fold_in(own_key, 6), dim), (blocks,), jnp.float32, least / len(cuts), top_value / len(cuts))
        return jnp.repeat(jnp.exp(steps), dims[dim] // blocks).reshape((-1,) + (1,) * (len(dims) - dim - 1))

    factor_of = one(*cuts[0])
    for cut in cuts[1:]:
        factor_of = factor_of * one(*cut)
    return factor_of


def gaussian(own_key, shape, spread, most, cuts=(), kind=jnp.bfloat16):
    gain = level_of(own_key, shape, cuts, -0.22, 0.18) if cuts else 1.0
    values = jax.random.normal(own_key, shape, jnp.float32) * spread * gain
    return jnp.minimum(jnp.maximum(values, -most), most).astype(kind)


def setup_inputs(seed: int = 0) -> dict:
    seeds = jax.random.split(jax.random.key(seed), 6)
    tokens = draw_tokens(jax.random.fold_in(seeds[5], 71), 0)
    w_query = draw_w_query(jax.random.fold_in(seeds[5], 71), 0)
    w_key = draw_w_key(jax.random.fold_in(seeds[5], 71), 0)
    w_value = gaussian(seeds[3], (D, D), D ** -0.5, 0.125, ((1, 8),))
    w_out = gaussian(seeds[4], (D, D), D ** -0.5, 0.125, ((0, 8),))
    return {"tokens": tokens, "w_query": w_query, "w_key": w_key, "w_value": w_value, "w_out": w_out}


LN_TWO = math.log(2.0)

def coarsen(array, factor):
    wide = array.astype(jnp.float32)
    return wide.reshape((wide.shape[0] // factor, factor) + wide.shape[1:]).mean(axis=1)

def sibling_blocks(array):
    count = array.shape[0]
    paired = array.reshape((count // 2, 2) + array.shape[1:])
    return jnp.flip(paired, axis=1).reshape(array.shape)

def near_field(query_rows, key_rows, value_rows):
    both_keys = jnp.concatenate([key_rows, sibling_blocks(key_rows)], axis=1)
    both_values = jnp.concatenate([value_rows, sibling_blocks(value_rows)], axis=1)
    scale_factor = 1.0 / math.sqrt(HEAD_DIM)
    score_matrix = jnp.einsum('ogxt,opxt->oxgp', query_rows.astype(jnp.float32), both_keys.astype(jnp.float32)) * scale_factor
    top = lax.optimization_barrier(jnp.max(score_matrix, axis=-1))
    weights = jnp.exp(score_matrix - top[..., None])
    total = lax.optimization_barrier(jnp.sum(weights, axis=-1))
    rounded = weights.astype(jnp.bfloat16)
    summed = jnp.einsum('bhqk,bkhd->bqhd', rounded.astype(jnp.float32), both_values.astype(jnp.float32))
    rows = query_rows.shape[0] * query_rows.shape[1]
    top = jnp.transpose(top, (0, 2, 1)).reshape(rows, query_rows.shape[2])
    total = jnp.transpose(total, (0, 2, 1)).reshape(rows, query_rows.shape[2])
    return (top, total, summed.reshape(rows, query_rows.shape[2], query_rows.shape[3]))

def distant_field(query_rows, key_rows, value_rows, extra_score):
    scale_factor = 1.0 / math.sqrt(HEAD_DIM)
    score_matrix = jnp.einsum('ogxt,opxt->oxgp', query_rows, key_rows, precision=lax.Precision.HIGHEST) * scale_factor + extra_score
    top = lax.optimization_barrier(jnp.max(score_matrix, axis=-1))
    weights = jnp.exp(score_matrix - top[..., None])
    total = lax.optimization_barrier(jnp.sum(weights, axis=-1))
    summed = jnp.einsum('bhqk,bkhd->bqhd', weights, value_rows, precision=lax.Precision.HIGHEST)
    rows = query_rows.shape[0] * query_rows.shape[1]
    top = jnp.transpose(top, (0, 2, 1)).reshape(rows, query_rows.shape[2])
    total = jnp.transpose(total, (0, 2, 1)).reshape(rows, query_rows.shape[2])
    return (top, total, summed.reshape(rows, query_rows.shape[2], query_rows.shape[3]))

def expand(part, factor):
    return tuple((jnp.repeat(member, factor, axis=0) for member in part))

def merge_level(state, part):
    newest = jnp.maximum(state[0], part[0])
    old_factor = jnp.exp(state[0] - newest)
    new_factor = jnp.exp(part[0] - newest)
    total = state[1] * old_factor + part[1] * new_factor
    summed = state[2] * old_factor[..., None] + part[2] * new_factor[..., None]
    return (newest, total, summed)

def head_attention(packed):
    query_rows, key_rows, value_rows = packed
    blocks = TOKENS // LEAF
    state = near_field(query_rows.reshape(blocks, LEAF, 1, HEAD_DIM), key_rows.reshape(blocks, LEAF, 1, HEAD_DIM), value_rows.reshape(blocks, LEAF, 1, HEAD_DIM))
    levels = blocks.bit_length() - 1
    for level in range(1, levels):
        factor = 2 ** level
        coarse_query = coarsen(query_rows, factor).reshape(-1, LEAF, 1, HEAD_DIM)
        coarse_keys = sibling_blocks(coarsen(key_rows, factor).reshape(-1, LEAF, 1, HEAD_DIM))
        coarse_values = sibling_blocks(coarsen(value_rows, factor).reshape(-1, LEAF, 1, HEAD_DIM))
        part = distant_field(coarse_query, coarse_keys, coarse_values, level * LN_TWO)
        state = merge_level(state, expand(part, factor))
    return state[2] / state[1][..., None]

def reference(tokens, w_query, w_key, w_value, w_out):

    def project(weight):
        result = jnp.dot(tokens, weight, preferred_element_type=jnp.float32).astype(jnp.bfloat16)
        return jnp.transpose(result.reshape(TOKENS, HEADS, HEAD_DIM), (1, 0, 2))[:, :, None, :]
    query_rows, key_rows, value_rows = (project(w_query), project(w_key), project(w_value))
    outputs = lax.map(head_attention, (query_rows, key_rows, value_rows))
    attention = jnp.transpose(outputs[:, :, 0, :], (1, 0, 2)).reshape(TOKENS, D).astype(jnp.bfloat16)
    return jnp.dot(attention, w_out, preferred_element_type=jnp.float32).astype(jnp.bfloat16)
```

```python
import functools
import math

import jax
import jax.numpy as jnp
from jax import lax
from jax.experimental import pallas as pl
from jax.experimental.pallas import tpu as pltpu
from jax.sharding import PartitionSpec as P

HEAD_DIM = 128
ROWS = 256
WIDTH = 256
MODEL = 2048
HALF = MODEL // 2
LEVELS = 5
SEQ = 32
RING = 8
PIECE = ROWS // RING
LOG2_E = 1.4426950408889634
SCORE_SCALE = LOG2_E / math.sqrt(HEAD_DIM)
MESH = pl.DeviceIdType.MESH
BF16 = jnp.bfloat16
F32 = jnp.float32


def dot(a, b):
    return jnp.dot(a, b, preferred_element_type=F32)


def dot_nt(a, b):
    return lax.dot_general(a, b, (((1,), (1,)), ((), ())), preferred_element_type=F32)


def averaging_rows(level):
    row = lax.broadcasted_iota(jnp.int32, (ROWS, ROWS), 0)
    col = lax.broadcasted_iota(jnp.int32, (ROWS, ROWS), 1)
    same = (row >> level) == (col >> level)
    return jnp.where(same, 2.0**-level, 0.0).astype(BF16)


def coarse_matrix():
    row = lax.broadcasted_iota(jnp.int32, (ROWS, ROWS), 0)
    col = lax.broadcasted_iota(jnp.int32, (ROWS, ROWS), 1)
    total = jnp.zeros((ROWS, ROWS), F32)
    start = 0
    for level in range(1, LEVELS + 1):
        count = ROWS >> level
        hit = (row >= start) & (row < start + count) & ((col >> level) == row - start)
        total = jnp.where(hit, 2.0**-level, total)
        start += count
    return total.astype(BF16)


def kernel(
    tok_hbm, wq_hbm, wk_hbm, wv_hbm, wo_hbm, out_ref,
    tok, wq, wk, wv, wo,
    send1, send2, send3, send4, send5,
    land1, land2, land3, land4, land5,
    partial, stage, ring,
    load_sem, send_sem, recv_sem, ring_send, ring_recv,
):
    sends = (send1, send2, send3, send4, send5)
    lands = (land1, land2, land3, land4, land5)
    me = lax.axis_index("seq")
    z = lax.axis_index("head")

    loads = [
        pltpu.make_async_copy(src, dst, load_sem.at[i])
        for i, (src, dst) in enumerate(
            ((tok_hbm, tok), (wk_hbm, wk), (wv_hbm, wv), (wq_hbm, wq), (wo_hbm, wo))
        )
    ]
    for load in loads:
        load.start()

    barrier = pltpu.get_barrier_semaphore()

    def greet(step, carry):
        pl.semaphore_signal(
            barrier, inc=1, device_id={"seq": (me + step) % SEQ}, device_id_type=MESH
        )
        return carry

    lax.fori_loop(1, SEQ, greet, 0)
    up, down = (z + 1) % RING, (z + RING - 1) % RING
    for neighbour in (up, down):
        pl.semaphore_signal(barrier, inc=1, device_id={"head": neighbour}, device_id_type=MESH)

    averages = coarse_matrix()
    loads[0].wait()
    loads[1].wait()
    key = dot(tok[...], wk[...]).astype(BF16)
    loads[2].wait()
    value = dot(tok[...], wv[...]).astype(BF16)
    coarse_key = dot(averages, key)
    coarse_value = dot(averages, value)
    start = 0
    for level in range(1, LEVELS + 1):
        count = ROWS >> level
        rows = slice(start, start + count)
        sends[level - 1][...] = jnp.concatenate(
            [coarse_key[rows], coarse_value[rows]], axis=0
        ).astype(BF16)
        start += count

    pl.semaphore_wait(barrier, SEQ - 1 + 2)

    for level in range(LEVELS, 0, -1):
        many = 1 << (level - 1)
        first = ((me // many) ^ 1) * many
        slot = me % many

        def post(step, carry, level=level, many=many, first=first, slot=slot):
            pltpu.make_async_remote_copy(
                src_ref=sends[level - 1],
                dst_ref=lands[level - 1].at[slot],
                send_sem=send_sem.at[level - 1],
                recv_sem=recv_sem.at[level - 1],
                device_id={"seq": first + (step + slot) % many},
                device_id_type=MESH,
            ).start()
            return carry

        lax.fori_loop(0, many, post, 0)

    loads[3].wait()
    query = dot(tok[...], wq[...]).astype(BF16)
    fine = []
    for level in range(1, LEVELS + 1):
        wide = dot(averaging_rows(level), query)
        high = wide.astype(BF16)
        low = (wide - high.astype(F32)).astype(BF16)
        fine.append((high, low))

    states = []
    for head in range(2):
        cols = slice(head * HEAD_DIM, (head + 1) * HEAD_DIM)
        scores = dot_nt(query[:, cols], key[:, cols]) * SCORE_SCALE
        top = jnp.max(scores, axis=1, keepdims=True)
        weights = jnp.exp2(scores - top)
        total = jnp.sum(weights, axis=1, keepdims=True)
        states.append((top, total, dot(weights.astype(BF16), value[:, cols])))

    far_keys, far_values = [], []
    for level in range(1, LEVELS + 1):
        many = 1 << (level - 1)
        count = ROWS >> level
        pltpu.make_async_copy(lands[level - 1], lands[level - 1], recv_sem.at[level - 1]).wait()
        if count >= 16:
            block = lands[level - 1][...]
        else:
            block = lands[level - 1][...].astype(F32)
        far_keys.append(block[:, :count, :].reshape(many * count, WIDTH).astype(BF16))
        far_values.append(block[:, count:, :].reshape(many * count, WIDTH).astype(BF16))

    mixed = []
    for head in range(2):
        cols = slice(head * HEAD_DIM, (head + 1) * HEAD_DIM)
        parts = []
        for level in range(1, LEVELS + 1):
            high, low = fine[level - 1]
            left = jnp.concatenate([high[:, cols], low[:, cols]], axis=1)
            right = far_keys[level - 1][:, cols]
            right = jnp.concatenate([right, right], axis=1)
            parts.append(dot_nt(left, right) * SCORE_SCALE + float(level))
        scores = jnp.concatenate(parts, axis=1)
        top, total, summed = states[head]
        newest = jnp.maximum(top, jnp.max(scores, axis=1, keepdims=True))
        old = jnp.exp2(top - newest)
        weights = jnp.exp2(scores - newest)
        values = jnp.concatenate([block[:, cols] for block in far_values], axis=0)
        total = total * old + jnp.sum(weights, axis=1, keepdims=True)
        summed = summed * old + dot(weights.astype(BF16), values)
        mixed.append((summed / total).astype(BF16))
    attention = jnp.concatenate(mixed, axis=1)

    loads[4].wait()

    def hop(way, chain, number):
        index = way * 7 + (number if chain == 0 else 4 + number)
        return pltpu.make_async_remote_copy(
            src_ref=stage.at[index],
            dst_ref=ring.at[index],
            send_sem=ring_send.at[index],
            recv_sem=ring_recv.at[index],
            device_id={"head": up if way == 0 else down},
            device_id_type=MESH,
        ), index

    def own(way, chain, distance):
        half = way if chain == 0 else 1 - way
        target = (z + distance) % RING if way == 0 else (z + RING - distance) % RING
        first = pl.multiple_of(target * PIECE, PIECE)
        return partial[pl.ds(first, PIECE), half * HALF:(half + 1) * HALF]

    hops = []

    def send(way, chain, number):
        copy, index = hop(way, chain, number)
        distance = 4 - number if chain == 0 else 3 - number
        term = own(way, chain, distance)
        if number > 0:
            before, previous = hop(way, chain, number - 1)
            before.wait_recv()
            term = term + ring[previous].astype(F32)
        stage[index] = term.astype(BF16)
        copy.start()
        hops.append(copy)

    for half in range(2):
        columns = slice(half * HALF, (half + 1) * HALF)
        partial[:, columns] = dot(attention, wo[:, columns])
        send(half, 0, 0)
    for way in range(2):
        send(way, 1, 0)
    for number in range(1, 4):
        for chain in range(2):
            if chain == 1 and number == 3:
                continue
            for way in range(2):
                send(way, chain, number)
    mine = pl.multiple_of(z * PIECE, PIECE)
    for half in range(2):
        other = 1 - half
        short, short_index = hop(other, 1, 2)
        long, long_index = hop(half, 0, 3)
        short.wait_recv()
        total = partial[pl.ds(mine, PIECE), half * HALF:(half + 1) * HALF]
        total = total + ring[short_index].astype(F32)
        long.wait_recv()
        total = total + ring[long_index].astype(F32)
        out_ref[:, half * HALF:(half + 1) * HALF] = total.astype(BF16)

    for copy in hops:
        copy.wait_send()
    for level in range(1, LEVELS + 1):
        pltpu.make_async_copy(lands[level - 1], lands[level - 1], send_sem.at[level - 1]).wait()


def shards(tokens, w_query, w_key, w_value, w_out):
    message = [(2 * (ROWS >> level), WIDTH) for level in range(1, LEVELS + 1)]
    return pl.pallas_call(
        kernel,
        out_shape=jax.ShapeDtypeStruct((PIECE, MODEL), BF16),
        in_specs=[pl.BlockSpec(memory_space=pl.ANY)] * 5,
        out_specs=pl.BlockSpec(memory_space=pltpu.VMEM),
        scratch_shapes=[
            pltpu.VMEM((ROWS, MODEL), BF16),
            pltpu.VMEM((MODEL, WIDTH), BF16),
            pltpu.VMEM((MODEL, WIDTH), BF16),
            pltpu.VMEM((MODEL, WIDTH), BF16),
            pltpu.VMEM((WIDTH, MODEL), BF16),
            *[pltpu.VMEM(shape, BF16) for shape in message],
            *[pltpu.VMEM((1 << i, *shape), BF16) for i, shape in enumerate(message)],
            pltpu.VMEM((ROWS, MODEL), F32),
            pltpu.VMEM((14, PIECE, HALF), BF16),
            pltpu.VMEM((14, PIECE, HALF), BF16),
            pltpu.SemaphoreType.DMA((5,)),
            pltpu.SemaphoreType.DMA((LEVELS,)),
            pltpu.SemaphoreType.DMA((LEVELS,)),
            pltpu.SemaphoreType.DMA((14,)),
            pltpu.SemaphoreType.DMA((14,)),
        ],
        compiler_params=pltpu.CompilerParams(
            collective_id=0, has_side_effects=True, vmem_limit_bytes=40 * 1024 * 1024
        ),
    )(tokens, w_query, w_key, w_value, w_out)


def solution(mesh):
    placed = (P("seq", None), P(None, "head"), P(None, "head"), P(None, "head"), P("head", None))
    return jax.shard_map(
        shards, mesh=mesh, in_specs=placed, out_specs=P(("seq", "head"), None), check_vma=False
    )
```

```python
import functools
import math

import jax
import jax.numpy as jnp
from jax import lax
from jax.experimental import pallas as pl
from jax.experimental.pallas import tpu as pltpu
from jax.sharding import PartitionSpec as P

HEAD_DIM = 128
ROWS = 256
WIDTH = 256
MODEL = 2048
HALF = MODEL // 2
PARTS = 1
COLS = HALF // PARTS
LEVELS = 5
FAR = LEVELS * HEAD_DIM
ORDER = (5, 4, 3, 2, 1)
FORWARD = (2, 3, 4, 5,)
SEQ = 32
RING = 8
PIECE = ROWS // RING
LOG2_E = 1.4426950408889634
SCORE_SCALE = LOG2_E / math.sqrt(HEAD_DIM)
MESH = pl.DeviceIdType.MESH
BF16 = jnp.bfloat16
F32 = jnp.float32
VMEM_BYTES = 107 * 512 * 1024


def dot(a, b):
    return jnp.dot(a, b, preferred_element_type=F32)


def dot_nt(a, b):
    return lax.dot_general(a, b, (((1,), (1,)), ((), ())), preferred_element_type=F32)


def averaging_rows(level):
    row = lax.broadcasted_iota(jnp.int32, (ROWS, ROWS), 0)
    col = lax.broadcasted_iota(jnp.int32, (ROWS, ROWS), 1)
    same = (row >> level) == (col >> level)
    return jnp.where(same, 2.0**-level, 0.0).astype(BF16)


def coarse_matrix():
    row = lax.broadcasted_iota(jnp.int32, (ROWS, ROWS), 0)
    col = lax.broadcasted_iota(jnp.int32, (ROWS, ROWS), 1)
    total = jnp.zeros((ROWS, ROWS), F32)
    start = 0
    for level in range(1, LEVELS + 1):
        count = ROWS >> level
        hit = (row >= start) & (row < start + count) & ((col >> level) == row - start)
        total = jnp.where(hit, 2.0**-level, total)
        start += count
    return total.astype(BF16)


def kernel(
    tok_hbm, wq_hbm, wk_hbm, wv_hbm, wo_hbm, out_ref,
    tok, wq, wk, wv, wo,
    send1, send2, send3, send4, send5,
    land1, land2, land3, land4, land5,
    fine, near_top, near_total, near_sum, far_key, far_value,
    partial, stage, ring,
    load_sem, send_sem, recv_sem, pass_send, pass_recv, ring_send, ring_recv,
):
    sends = (send1, send2, send3, send4, send5)
    lands = (land1, land2, land3, land4, land5)
    me = lax.axis_index("seq")
    z = lax.axis_index("head")
    core = me % 2

    loads = [
        pltpu.make_async_copy(src, dst, load_sem.at[i])
        for i, (src, dst) in enumerate(
            ((tok_hbm, tok), (wk_hbm, wk), (wv_hbm, wv), (wq_hbm, wq), (wo_hbm, wo))
        )
    ]
    for load in loads:
        load.start()

    barrier = pltpu.get_barrier_semaphore()

    def greet(step, carry):
        pl.semaphore_signal(
            barrier, inc=1, device_id={"seq": (me + step) % SEQ}, device_id_type=MESH
        )
        return carry

    lax.fori_loop(1, SEQ, greet, 0)
    up, down = (z + 1) % RING, (z + RING - 1) % RING
    for neighbour in (up, down):
        pl.semaphore_signal(barrier, inc=1, device_id={"head": neighbour}, device_id_type=MESH)

    averages = coarse_matrix()
    loads[0].wait()
    loads[1].wait()
    key = dot(tok[...], wk[...]).astype(BF16)
    loads[2].wait()
    value = dot(tok[...], wv[...]).astype(BF16)
    coarse_key = dot(averages, key)
    coarse_value = dot(averages, value)
    start = 0
    for level in range(1, LEVELS + 1):
        count = ROWS >> level
        rows = slice(start, start + count)
        sends[level - 1][...] = jnp.concatenate(
            [coarse_key[rows], coarse_value[rows]], axis=0
        ).astype(BF16)
        start += count

    pl.semaphore_wait(barrier, SEQ - 1 + 2)

    for level in ORDER:
        many = 1 << (level - 1)
        first = ((me // many) ^ 1) * many
        place = me % many
        slot = place if level == 1 else core * (many // 2) + place // 2
        step_of = 2 if level in FORWARD else 1

        def post(step, carry, level=level, many=many, first=first, place=place, slot=slot, by=step_of):
            pltpu.make_async_remote_copy(
                src_ref=sends[level - 1],
                dst_ref=lands[level - 1].at[slot],
                send_sem=send_sem.at[level - 1],
                recv_sem=recv_sem.at[level - 1],
                device_id={"seq": first + (by * step + place) % many},
                device_id_type=MESH,
            ).start()
            return carry

        lax.fori_loop(0, many // step_of, post, 0)

    loads[3].wait()
    query = dot(tok[...], wq[...]).astype(BF16)
    for level in range(1, LEVELS + 1):
        wide = dot(averaging_rows(level), query)
        high = wide.astype(BF16)
        low = (wide - high.astype(F32)).astype(BF16)
        for head in range(2):
            cols = slice(head * HEAD_DIM, (head + 1) * HEAD_DIM)
            fine[level - 1, head, :, :HEAD_DIM] = high[:, cols]
            fine[level - 1, head, :, HEAD_DIM:] = low[:, cols]

    for head in range(2):
        cols = slice(head * HEAD_DIM, (head + 1) * HEAD_DIM)
        scores = dot_nt(query[:, cols], key[:, cols]) * SCORE_SCALE
        top = jnp.max(scores, axis=1, keepdims=True)
        weights = jnp.exp2(scores - top)
        total = jnp.sum(weights, axis=1, keepdims=True)
        near_top[head] = jnp.broadcast_to(top, (ROWS, HEAD_DIM))
        near_total[head] = jnp.broadcast_to(total, (ROWS, HEAD_DIM))
        near_sum[head] = dot(weights.astype(BF16), value[:, cols])

    def received(level):
        return lands[level - 1].at[pl.ds(core * (1 << (level - 2)), 1 << (level - 2))]

    def passed(level):
        return lands[level - 1].at[pl.ds((1 - core) * (1 << (level - 2)), 1 << (level - 2))]

    def handover(level):
        return pltpu.make_async_remote_copy(
            src_ref=received(level),
            dst_ref=received(level),
            send_sem=pass_send.at[level - 1],
            recv_sem=pass_recv.at[level - 1],
            device_id={"seq": me ^ 1},
            device_id_type=MESH,
        )

    for level in FORWARD:
        pltpu.make_async_copy(received(level), received(level), recv_sem.at[level - 1]).wait()
        handover(level).start()

    for level in range(1, LEVELS + 1):
        many = 1 << (level - 1)
        count = ROWS >> level
        if level in FORWARD:
            pltpu.make_async_copy(passed(level), passed(level), pass_recv.at[level - 1]).wait()
        else:
            pltpu.make_async_copy(lands[level - 1], lands[level - 1], recv_sem.at[level - 1]).wait()
        block = lands[level - 1][...]
        if count < 16:
            block = block.astype(F32)
        keys = block[:, :count, :].reshape(many * count, WIDTH).astype(BF16)
        values = block[:, count:, :].reshape(many * count, WIDTH).astype(BF16)
        rows = slice((level - 1) * HEAD_DIM, level * HEAD_DIM)
        for head in range(2):
            cols = slice(head * HEAD_DIM, (head + 1) * HEAD_DIM)
            far_key[head, rows, :HEAD_DIM] = keys[:, cols]
            far_key[head, rows, HEAD_DIM:] = keys[:, cols]
            far_value[head, rows, :] = values[:, cols]

    def attend(rows):
        mixed = []
        for head in range(2):
            parts = []
            for level in range(1, LEVELS + 1):
                section = slice((level - 1) * HEAD_DIM, level * HEAD_DIM)
                product = dot_nt(fine[level - 1, head, rows, :], far_key[head, section, :])
                parts.append(product * SCORE_SCALE + float(level))
            scores = jnp.concatenate(parts, axis=1)
            top = near_top[head, rows, :][:, :1]
            newest = jnp.maximum(top, jnp.max(scores, axis=1, keepdims=True))
            old = jnp.exp2(top - newest)
            weights = jnp.exp2(scores - newest)
            total = near_total[head, rows, :][:, :1] * old + jnp.sum(weights, axis=1, keepdims=True)
            summed = near_sum[head, rows, :] * old + dot(weights.astype(BF16), far_value[head])
            mixed.append((summed / total).astype(BF16))
        return jnp.concatenate(mixed, axis=1)

    def hop(way, chain, part, number):
        index = (way * 7 + (number if chain == 0 else 4 + number)) * PARTS + part
        return pltpu.make_async_remote_copy(
            src_ref=stage.at[index],
            dst_ref=ring.at[index],
            send_sem=ring_send.at[index],
            recv_sem=ring_recv.at[index],
            device_id={"head": up if way == 0 else down},
            device_id_type=MESH,
        ), index

    def columns_of(half, part):
        first = half * HALF + part * COLS
        return slice(first, first + COLS)

    def own(way, chain, part, distance):
        half = way if chain == 0 else 1 - way
        target = (z + distance) % RING if way == 0 else (z + RING - distance) % RING
        first = pl.multiple_of(target * PIECE, PIECE)
        return partial[pl.ds(first, PIECE), columns_of(half, part)]

    hops = []

    def send(way, chain, part, number):
        copy, index = hop(way, chain, part, number)
        term = own(way, chain, part, 4 - number if chain == 0 else 3 - number)
        if number > 0:
            before, previous = hop(way, chain, part, number - 1)
            before.wait_recv()
            term = term + ring[previous].astype(F32)
        stage[index] = term.astype(BF16)
        copy.start()
        hops.append(copy)

    loads[4].wait()
    opposite = pl.ds(pl.multiple_of(((z + RING // 2) % RING) * PIECE, PIECE), PIECE)
    attention = attend(opposite)
    for part in range(PARTS):
        for way in range(2):
            copy, index = hop(way, 0, part, 0)
            stage[index] = dot(attention, wo[:, columns_of(way, part)]).astype(BF16)
            copy.start()
            hops.append(copy)

    partial[...] = dot(attend(slice(0, ROWS)), wo[...])
    for part in range(PARTS):
        for way in range(2):
            send(way, 1, part, 0)
    for number in range(1, 4):
        for chain in range(2):
            if chain == 1 and number == 3:
                continue
            for part in range(PARTS):
                for way in range(2):
                    send(way, chain, part, number)
    mine = pl.multiple_of(z * PIECE, PIECE)
    for part in range(PARTS):
        for half in range(2):
            columns = columns_of(half, part)
            short, short_index = hop(1 - half, 1, part, 2)
            long, long_index = hop(half, 0, part, 3)
            short.wait_recv()
            total = partial[pl.ds(mine, PIECE), columns]
            total = total + ring[short_index].astype(F32)
            long.wait_recv()
            total = total + ring[long_index].astype(F32)
            out_ref[:, columns] = total.astype(BF16)

    for copy in hops:
        copy.wait_send()
    for level in range(1, LEVELS + 1):
        if level in FORWARD:
            handover(level).wait_send()
            pltpu.make_async_copy(received(level), received(level), send_sem.at[level - 1]).wait()
        else:
            pltpu.make_async_copy(lands[level - 1], lands[level - 1], send_sem.at[level - 1]).wait()


def shards(tokens, w_query, w_key, w_value, w_out):
    message = [(2 * (ROWS >> level), WIDTH) for level in range(1, LEVELS + 1)]
    return pl.pallas_call(
        kernel,
        out_shape=jax.ShapeDtypeStruct((PIECE, MODEL), BF16),
        in_specs=[pl.BlockSpec(memory_space=pl.ANY)] * 5,
        out_specs=pl.BlockSpec(memory_space=pltpu.VMEM),
        scratch_shapes=[
            pltpu.VMEM((ROWS, MODEL), BF16),
            pltpu.VMEM((MODEL, WIDTH), BF16),
            pltpu.VMEM((MODEL, WIDTH), BF16),
            pltpu.VMEM((MODEL, WIDTH), BF16),
            pltpu.VMEM((WIDTH, MODEL), BF16),
            *[pltpu.VMEM(shape, BF16) for shape in message],
            *[pltpu.VMEM((1 << i, *shape), BF16) for i, shape in enumerate(message)],
            pltpu.VMEM((LEVELS, 2, ROWS, 2 * HEAD_DIM), BF16),
            pltpu.VMEM((2, ROWS, HEAD_DIM), F32),
            pltpu.VMEM((2, ROWS, HEAD_DIM), F32),
            pltpu.VMEM((2, ROWS, HEAD_DIM), F32),
            pltpu.VMEM((2, FAR, 2 * HEAD_DIM), BF16),
            pltpu.VMEM((2, FAR, HEAD_DIM), BF16),
            pltpu.VMEM((ROWS, MODEL), F32),
            pltpu.VMEM((14 * PARTS, PIECE, COLS), BF16),
            pltpu.VMEM((14 * PARTS, PIECE, COLS), BF16),
            pltpu.SemaphoreType.DMA((5,)),
            pltpu.SemaphoreType.DMA((LEVELS,)),
            pltpu.SemaphoreType.DMA((LEVELS,)),
            pltpu.SemaphoreType.DMA((LEVELS,)),
            pltpu.SemaphoreType.DMA((LEVELS,)),
            pltpu.SemaphoreType.DMA((14 * PARTS,)),
            pltpu.SemaphoreType.DMA((14 * PARTS,)),
        ],
        compiler_params=pltpu.CompilerParams(
            collective_id=0, has_side_effects=True, vmem_limit_bytes=VMEM_BYTES
        ),
    )(tokens, w_query, w_key, w_value, w_out)


def solution(mesh):
    placed = (P("seq", None), P(None, "head"), P(None, "head"), P(None, "head"), P("head", None))
    return jax.shard_map(
        shards, mesh=mesh, in_specs=placed, out_specs=P(("seq", "head"), None), check_vma=False
    )
```

```python
import functools
import math

import jax
import jax.numpy as jnp
from jax import lax
from jax.experimental import pallas as pl
from jax.experimental.pallas import tpu as pltpu
from jax.sharding import PartitionSpec as P

HEAD_DIM = 128
ROWS = 256
WIDTH = 256
MODEL = 2048
HALF = MODEL // 2
PARTS = 1
COLS = HALF // PARTS
LEVELS = 5
FAR = LEVELS * HEAD_DIM
ORDER = (5, 4, 3, 2, 1)
FORWARD = (2, 3, 4, 5,)
SEQ = 32
RING = 8
PIECE = ROWS // RING
LOG2_E = 1.4426950408889634
SCORE_SCALE = LOG2_E / math.sqrt(HEAD_DIM)
MESH = pl.DeviceIdType.MESH
BF16 = jnp.bfloat16
F32 = jnp.float32
VMEM_BYTES = 107 * 512 * 1024


def dot(a, b):
    return jnp.dot(a, b, preferred_element_type=F32)


def dot_nt(a, b):
    return lax.dot_general(a, b, (((1,), (1,)), ((), ())), preferred_element_type=F32)


def averaging_rows(level):
    row = lax.broadcasted_iota(jnp.int32, (ROWS, ROWS), 0)
    col = lax.broadcasted_iota(jnp.int32, (ROWS, ROWS), 1)
    same = (row >> level) == (col >> level)
    return jnp.where(same, 2.0**-level, 0.0).astype(BF16)


def coarse_matrix():
    row = lax.broadcasted_iota(jnp.int32, (ROWS, ROWS), 0)
    col = lax.broadcasted_iota(jnp.int32, (ROWS, ROWS), 1)
    total = jnp.zeros((ROWS, ROWS), F32)
    start = 0
    for level in range(1, LEVELS + 1):
        count = ROWS >> level
        hit = (row >= start) & (row < start + count) & ((col >> level) == row - start)
        total = jnp.where(hit, 2.0**-level, total)
        start += count
    return total.astype(BF16)


def kernel(
    tok_hbm, wq_hbm, wk_hbm, wv_hbm, wo_hbm, out_ref,
    tok, wq, wk, wv, wo,
    send1, send2, send3, send4, send5,
    land1, land2, land3, land4, land5,
    fine, near_top, near_total, near_sum, far_key, far_value,
    partial, stage, ring,
    load_sem, send_sem, recv_sem, pass_send, pass_recv, ring_send, ring_recv,
):
    sends = (send1, send2, send3, send4, send5)
    lands = (land1, land2, land3, land4, land5)
    me = lax.axis_index("seq")
    z = lax.axis_index("head")
    core = me % 2

    barrier = pltpu.get_barrier_semaphore()

    def greet(step, carry):
        pl.semaphore_signal(
            barrier, inc=1, device_id={"seq": (me + step) % SEQ}, device_id_type=MESH
        )
        return carry

    lax.fori_loop(1, SEQ, greet, 0)
    up, down = (z + 1) % RING, (z + RING - 1) % RING
    for neighbour in (up, down):
        pl.semaphore_signal(barrier, inc=1, device_id={"head": neighbour}, device_id_type=MESH)

    loads = [
        pltpu.make_async_copy(src, dst, load_sem.at[i])
        for i, (src, dst) in enumerate(
            ((tok_hbm, tok), (wk_hbm, wk), (wv_hbm, wv), (wq_hbm, wq), (wo_hbm, wo))
        )
    ]
    for load in loads:
        load.start()

    averages = coarse_matrix()
    loads[0].wait()
    loads[1].wait()
    key = dot(tok[...], wk[...]).astype(BF16)
    loads[2].wait()
    value = dot(tok[...], wv[...]).astype(BF16)
    coarse_key = dot(averages, key)
    coarse_value = dot(averages, value)
    start = 0
    for level in range(1, LEVELS + 1):
        count = ROWS >> level
        rows = slice(start, start + count)
        sends[level - 1][...] = jnp.concatenate(
            [coarse_key[rows], coarse_value[rows]], axis=0
        ).astype(BF16)
        start += count

    pl.semaphore_wait(barrier, SEQ - 1 + 2)

    for level in ORDER:
        many = 1 << (level - 1)
        first = ((me // many) ^ 1) * many
        place = me % many
        slot = place if level == 1 else core * (many // 2) + place // 2
        step_of = 2 if level in FORWARD else 1

        def post(step, carry, level=level, many=many, first=first, place=place, slot=slot, by=step_of):
            pltpu.make_async_remote_copy(
                src_ref=sends[level - 1],
                dst_ref=lands[level - 1].at[slot],
                send_sem=send_sem.at[level - 1],
                recv_sem=recv_sem.at[level - 1],
                device_id={"seq": first + (by * step + place) % many},
                device_id_type=MESH,
            ).start()
            return carry

        lax.fori_loop(0, many // step_of, post, 0)

    loads[3].wait()
    query = dot(tok[...], wq[...]).astype(BF16)
    for level in range(1, LEVELS + 1):
        wide = dot(averaging_rows(level), query)
        high = wide.astype(BF16)
        low = (wide - high.astype(F32)).astype(BF16)
        for head in range(2):
            cols = slice(head * HEAD_DIM, (head + 1) * HEAD_DIM)
            fine[level - 1, head, :, :HEAD_DIM] = high[:, cols]
            fine[level - 1, head, :, HEAD_DIM:] = low[:, cols]

    for head in range(2):
        cols = slice(head * HEAD_DIM, (head + 1) * HEAD_DIM)
        scores = dot_nt(query[:, cols], key[:, cols]) * SCORE_SCALE
        top = jnp.max(scores, axis=1, keepdims=True)
        weights = jnp.exp2(scores - top)
        total = jnp.sum(weights, axis=1, keepdims=True)
        near_top[head] = jnp.broadcast_to(top, (ROWS, HEAD_DIM))
        near_total[head] = jnp.broadcast_to(total, (ROWS, HEAD_DIM))
        near_sum[head] = dot(weights.astype(BF16), value[:, cols])

    def received(level):
        return lands[level - 1].at[pl.ds(core * (1 << (level - 2)), 1 << (level - 2))]

    def passed(level):
        return lands[level - 1].at[pl.ds((1 - core) * (1 << (level - 2)), 1 << (level - 2))]

    def handover(level):
        return pltpu.make_async_remote_copy(
            src_ref=received(level),
            dst_ref=received(level),
            send_sem=pass_send.at[level - 1],
            recv_sem=pass_recv.at[level - 1],
            device_id={"seq": me ^ 1},
            device_id_type=MESH,
        )

    def take(level, slots, place):
        count = ROWS >> level
        block = lands[level - 1][slots]
        if count < 16:
            block = block.astype(F32)
        length = block.shape[0] * count
        keys = block[:, :count, :].reshape(length, WIDTH).astype(BF16)
        values = block[:, count:, :].reshape(length, WIDTH).astype(BF16)
        rows = slice((level - 1) * HEAD_DIM + place, (level - 1) * HEAD_DIM + place + length)
        for head in range(2):
            cols = slice(head * HEAD_DIM, (head + 1) * HEAD_DIM)
            far_key[head, rows, :HEAD_DIM] = keys[:, cols]
            far_key[head, rows, HEAD_DIM:] = keys[:, cols]
            far_value[head, rows, :] = values[:, cols]

    for level in (4, 5, 3, 2):
        pltpu.make_async_copy(received(level), received(level), recv_sem.at[level - 1]).wait()
        handover(level).start()
    pltpu.make_async_copy(land1, land1, recv_sem.at[0]).wait()
    take(1, slice(0, 1), 0)
    for level in FORWARD:
        take(level, pl.ds(core * (1 << (level - 2)), 1 << (level - 2)), 0)
    for level in (4, 5, 3, 2):
        pltpu.make_async_copy(passed(level), passed(level), pass_recv.at[level - 1]).wait()
        take(level, pl.ds((1 - core) * (1 << (level - 2)), 1 << (level - 2)), HEAD_DIM // 2)

    def attend(rows):
        mixed = []
        for head in range(2):
            parts = []
            for level in range(1, LEVELS + 1):
                section = slice((level - 1) * HEAD_DIM, level * HEAD_DIM)
                product = dot_nt(fine[level - 1, head, rows, :], far_key[head, section, :])
                parts.append(product * SCORE_SCALE + float(level))
            scores = jnp.concatenate(parts, axis=1)
            top = near_top[head, rows, :][:, :1]
            newest = jnp.maximum(top, jnp.max(scores, axis=1, keepdims=True))
            old = jnp.exp2(top - newest)
            weights = jnp.exp2(scores - newest)
            total = near_total[head, rows, :][:, :1] * old + jnp.sum(weights, axis=1, keepdims=True)
            summed = near_sum[head, rows, :] * old + dot(weights.astype(BF16), far_value[head])
            mixed.append((summed / total).astype(BF16))
        return jnp.concatenate(mixed, axis=1)

    def hop(way, chain, part, number):
        index = (way * 7 + (number if chain == 0 else 4 + number)) * PARTS + part
        return pltpu.make_async_remote_copy(
            src_ref=stage.at[index],
            dst_ref=ring.at[index],
            send_sem=ring_send.at[index],
            recv_sem=ring_recv.at[index],
            device_id={"head": up if way == 0 else down},
            device_id_type=MESH,
        ), index

    def columns_of(half, part):
        first = half * HALF + part * COLS
        return slice(first, first + COLS)

    def own(way, chain, part, distance):
        half = way if chain == 0 else 1 - way
        target = (z + distance) % RING if way == 0 else (z + RING - distance) % RING
        first = pl.multiple_of(target * PIECE, PIECE)
        return partial[pl.ds(first, PIECE), columns_of(half, part)]

    hops = []

    def send(way, chain, part, number):
        copy, index = hop(way, chain, part, number)
        term = own(way, chain, part, 4 - number if chain == 0 else 3 - number)
        if number > 0:
            before, previous = hop(way, chain, part, number - 1)
            before.wait_recv()
            term = term + ring[previous].astype(F32)
        stage[index] = term.astype(BF16)
        copy.start()
        hops.append(copy)

    loads[4].wait()
    opposite = pl.ds(pl.multiple_of(((z + RING // 2) % RING) * PIECE, PIECE), PIECE)
    attention = attend(opposite)
    for part in range(PARTS):
        for way in range(2):
            copy, index = hop(way, 0, part, 0)
            stage[index] = dot(attention, wo[:, columns_of(way, part)]).astype(BF16)
            copy.start()
            hops.append(copy)

    partial[...] = dot(attend(slice(0, ROWS)), wo[...])
    for part in range(PARTS):
        for way in range(2):
            send(way, 1, part, 0)
    for number in range(1, 4):
        for chain in range(2):
            if chain == 1 and number == 3:
                continue
            for part in range(PARTS):
                for way in range(2):
                    send(way, chain, part, number)
    mine = pl.multiple_of(z * PIECE, PIECE)
    for part in range(PARTS):
        for half in range(2):
            columns = columns_of(half, part)
            short, short_index = hop(1 - half, 1, part, 2)
            long, long_index = hop(half, 0, part, 3)
            short.wait_recv()
            total = partial[pl.ds(mine, PIECE), columns]
            total = total + ring[short_index].astype(F32)
            long.wait_recv()
            total = total + ring[long_index].astype(F32)
            out_ref[:, columns] = total.astype(BF16)

    for copy in hops:
        copy.wait_send()
    for level in range(1, LEVELS + 1):
        if level in FORWARD:
            handover(level).wait_send()
            pltpu.make_async_copy(received(level), received(level), send_sem.at[level - 1]).wait()
        else:
            pltpu.make_async_copy(lands[level - 1], lands[level - 1], send_sem.at[level - 1]).wait()


def shards(tokens, w_query, w_key, w_value, w_out):
    message = [(2 * (ROWS >> level), WIDTH) for level in range(1, LEVELS + 1)]
    return pl.pallas_call(
        kernel,
        out_shape=jax.ShapeDtypeStruct((PIECE, MODEL), BF16),
        in_specs=[pl.BlockSpec(memory_space=pl.ANY)] * 5,
        out_specs=pl.BlockSpec(memory_space=pltpu.VMEM),
        scratch_shapes=[
            pltpu.VMEM((ROWS, MODEL), BF16),
            pltpu.VMEM((MODEL, WIDTH), BF16),
            pltpu.VMEM((MODEL, WIDTH), BF16),
            pltpu.VMEM((MODEL, WIDTH), BF16),
            pltpu.VMEM((WIDTH, MODEL), BF16),
            *[pltpu.VMEM(shape, BF16) for shape in message],
            *[pltpu.VMEM((1 << i, *shape), BF16) for i, shape in enumerate(message)],
            pltpu.VMEM((LEVELS, 2, ROWS, 2 * HEAD_DIM), BF16),
            pltpu.VMEM((2, ROWS, HEAD_DIM), F32),
            pltpu.VMEM((2, ROWS, HEAD_DIM), F32),
            pltpu.VMEM((2, ROWS, HEAD_DIM), F32),
            pltpu.VMEM((2, FAR, 2 * HEAD_DIM), BF16),
            pltpu.VMEM((2, FAR, HEAD_DIM), BF16),
            pltpu.VMEM((ROWS, MODEL), F32),
            pltpu.VMEM((14 * PARTS, PIECE, COLS), BF16),
            pltpu.VMEM((14 * PARTS, PIECE, COLS), BF16),
            pltpu.SemaphoreType.DMA((5,)),
            pltpu.SemaphoreType.DMA((LEVELS,)),
            pltpu.SemaphoreType.DMA((LEVELS,)),
            pltpu.SemaphoreType.DMA((LEVELS,)),
            pltpu.SemaphoreType.DMA((LEVELS,)),
            pltpu.SemaphoreType.DMA((14 * PARTS,)),
            pltpu.SemaphoreType.DMA((14 * PARTS,)),
        ],
        compiler_params=pltpu.CompilerParams(
            collective_id=0, has_side_effects=True, vmem_limit_bytes=VMEM_BYTES
        ),
    )(tokens, w_query, w_key, w_value, w_out)


def solution(mesh):
    placed = (P("seq", None), P(None, "head"), P(None, "head"), P(None, "head"), P("head", None))
    return jax.shard_map(
        shards, mesh=mesh, in_specs=placed, out_specs=P(("seq", "head"), None), check_vma=False
    )
```

```python
import functools
import math

import jax
import jax.numpy as jnp
from jax import lax
from jax.experimental import pallas as pl
from jax.experimental.pallas import tpu as pltpu
from jax.sharding import PartitionSpec as P

HEAD_DIM = 128
ROWS = 256
WIDTH = 256
MODEL = 2048
HALF = MODEL // 2
PARTS = 1
COLS = HALF // PARTS
LEVELS = 5
FAR = LEVELS * HEAD_DIM
ORDER = (5, 4, 3, 2, 1)
FORWARD = (2, 3, 4, 5,)
CHUNKS = 4
DEPTH = MODEL // CHUNKS
SEQ = 32
RING = 8
PIECE = ROWS // RING
LOG2_E = 1.4426950408889634
SCORE_SCALE = LOG2_E / math.sqrt(HEAD_DIM)
MESH = pl.DeviceIdType.MESH
BF16 = jnp.bfloat16
F32 = jnp.float32
VMEM_BYTES = 107 * 512 * 1024


def dot(a, b):
    return jnp.dot(a, b, preferred_element_type=F32)


def dot_nt(a, b):
    return lax.dot_general(a, b, (((1,), (1,)), ((), ())), preferred_element_type=F32)


def averaging_rows(level):
    row = lax.broadcasted_iota(jnp.int32, (ROWS, ROWS), 0)
    col = lax.broadcasted_iota(jnp.int32, (ROWS, ROWS), 1)
    same = (row >> level) == (col >> level)
    return jnp.where(same, 2.0**-level, 0.0).astype(BF16)


def coarse_matrix():
    row = lax.broadcasted_iota(jnp.int32, (ROWS, ROWS), 0)
    col = lax.broadcasted_iota(jnp.int32, (ROWS, ROWS), 1)
    total = jnp.zeros((ROWS, ROWS), F32)
    start = 0
    for level in range(1, LEVELS + 1):
        count = ROWS >> level
        hit = (row >= start) & (row < start + count) & ((col >> level) == row - start)
        total = jnp.where(hit, 2.0**-level, total)
        start += count
    return total.astype(BF16)


def kernel(
    tok_hbm, wq_hbm, wk_hbm, wv_hbm, wo_hbm, out_ref,
    tok, wq, wk, wv, wo,
    send1, send2, send3, send4, send5,
    land1, land2, land3, land4, land5,
    fine, near_top, near_total, near_sum, far_key, far_value,
    partial, stage, ring,
    load_sem, send_sem, recv_sem, pass_send, pass_recv, ring_send, ring_recv,
):
    sends = (send1, send2, send3, send4, send5)
    lands = (land1, land2, land3, land4, land5)
    me = lax.axis_index("seq")
    z = lax.axis_index("head")
    core = me % 2

    barrier = pltpu.get_barrier_semaphore()

    def greet(step, carry):
        pl.semaphore_signal(
            barrier, inc=1, device_id={"seq": (me + 2 * step) % SEQ}, device_id_type=MESH
        )
        return carry

    lax.fori_loop(1, SEQ // 2, greet, 0)
    pl.semaphore_signal(barrier, inc=1, device_id={"seq": me ^ 1}, device_id_type=MESH)
    up, down = (z + 1) % RING, (z + RING - 1) % RING
    for neighbour in (up, down):
        pl.semaphore_signal(barrier, inc=1, device_id={"head": neighbour}, device_id_type=MESH)

    loads = []
    for c in range(CHUNKS):
        span = pl.ds(c * DEPTH, DEPTH)
        for src, dst in (
            (tok_hbm.at[:, span], tok.at[:, span]),
            (wk_hbm.at[span], wk.at[span]),
            (wv_hbm.at[span], wv.at[span]),
        ):
            loads.append(pltpu.make_async_copy(src, dst, load_sem.at[len(loads)]))
    load_query = pltpu.make_async_copy(wq_hbm, wq, load_sem.at[3 * CHUNKS])
    load_out = pltpu.make_async_copy(wo_hbm, wo, load_sem.at[3 * CHUNKS + 1])
    for load in (*loads, load_query, load_out):
        load.start()

    averages = coarse_matrix()
    acc_key = jnp.zeros((ROWS, WIDTH), F32)
    acc_value = jnp.zeros((ROWS, WIDTH), F32)
    for c in range(CHUNKS):
        for load in loads[3 * c:3 * c + 3]:
            load.wait()
        span = slice(c * DEPTH, (c + 1) * DEPTH)
        acc_key += dot(tok[:, span], wk[span, :])
        acc_value += dot(tok[:, span], wv[span, :])
    key = acc_key.astype(BF16)
    value = acc_value.astype(BF16)
    coarse_key = dot(averages, key)
    coarse_value = dot(averages, value)
    start = 0
    for level in range(1, LEVELS + 1):
        count = ROWS >> level
        rows = slice(start, start + count)
        sends[level - 1][...] = jnp.concatenate(
            [coarse_key[rows], coarse_value[rows]], axis=0
        ).astype(BF16)
        start += count

    pl.semaphore_wait(barrier, SEQ // 2 - 1 + 1 + 2)

    for level in ORDER:
        many = 1 << (level - 1)
        first = ((me // many) ^ 1) * many
        place = me % many
        slot = place if level == 1 else core * (many // 2) + place // 2
        step_of = 2 if level in FORWARD else 1

        def post(step, carry, level=level, many=many, first=first, place=place, slot=slot, by=step_of):
            pltpu.make_async_remote_copy(
                src_ref=sends[level - 1],
                dst_ref=lands[level - 1].at[slot],
                send_sem=send_sem.at[level - 1],
                recv_sem=recv_sem.at[level - 1],
                device_id={"seq": first + (by * step + place) % many},
                device_id_type=MESH,
            ).start()
            return carry

        lax.fori_loop(0, many // step_of, post, 0)

    load_query.wait()
    query = dot(tok[...], wq[...]).astype(BF16)
    for level in range(1, LEVELS + 1):
        wide = dot(averaging_rows(level), query)
        high = wide.astype(BF16)
        low = (wide - high.astype(F32)).astype(BF16)
        for head in range(2):
            cols = slice(head * HEAD_DIM, (head + 1) * HEAD_DIM)
            fine[level - 1, head, :, :HEAD_DIM] = high[:, cols]
            fine[level - 1, head, :, HEAD_DIM:] = low[:, cols]

    for head in range(2):
        cols = slice(head * HEAD_DIM, (head + 1) * HEAD_DIM)
        scores = dot_nt(query[:, cols], key[:, cols]) * SCORE_SCALE
        top = jnp.max(scores, axis=1, keepdims=True)
        weights = jnp.exp2(scores - top)
        total = jnp.sum(weights, axis=1, keepdims=True)
        near_top[head] = jnp.broadcast_to(top, (ROWS, HEAD_DIM))
        near_total[head] = jnp.broadcast_to(total, (ROWS, HEAD_DIM))
        near_sum[head] = dot(weights.astype(BF16), value[:, cols])

    def received(level):
        return lands[level - 1].at[pl.ds(core * (1 << (level - 2)), 1 << (level - 2))]

    def passed(level):
        return lands[level - 1].at[pl.ds((1 - core) * (1 << (level - 2)), 1 << (level - 2))]

    def handover(level):
        return pltpu.make_async_remote_copy(
            src_ref=received(level),
            dst_ref=received(level),
            send_sem=pass_send.at[level - 1],
            recv_sem=pass_recv.at[level - 1],
            device_id={"seq": me ^ 1},
            device_id_type=MESH,
        )

    def take(level, slots, place):
        count = ROWS >> level
        block = lands[level - 1][slots]
        if count < 16:
            block = block.astype(F32)
        length = block.shape[0] * count
        keys = block[:, :count, :].reshape(length, WIDTH).astype(BF16)
        values = block[:, count:, :].reshape(length, WIDTH).astype(BF16)
        rows = slice((level - 1) * HEAD_DIM + place, (level - 1) * HEAD_DIM + place + length)
        for head in range(2):
            cols = slice(head * HEAD_DIM, (head + 1) * HEAD_DIM)
            far_key[head, rows, :HEAD_DIM] = keys[:, cols]
            far_key[head, rows, HEAD_DIM:] = keys[:, cols]
            far_value[head, rows, :] = values[:, cols]

    for level in (4, 5, 3, 2):
        pltpu.make_async_copy(received(level), received(level), recv_sem.at[level - 1]).wait()
        handover(level).start()
    pltpu.make_async_copy(land1, land1, recv_sem.at[0]).wait()
    take(1, slice(0, 1), 0)
    for level in FORWARD:
        take(level, pl.ds(core * (1 << (level - 2)), 1 << (level - 2)), 0)
    for level in (4, 5, 3, 2):
        pltpu.make_async_copy(passed(level), passed(level), pass_recv.at[level - 1]).wait()
        take(level, pl.ds((1 - core) * (1 << (level - 2)), 1 << (level - 2)), HEAD_DIM // 2)

    def attend(rows):
        mixed = []
        for head in range(2):
            parts = []
            for level in range(1, LEVELS + 1):
                section = slice((level - 1) * HEAD_DIM, level * HEAD_DIM)
                product = dot_nt(fine[level - 1, head, rows, :], far_key[head, section, :])
                parts.append(product * SCORE_SCALE + float(level))
            scores = jnp.concatenate(parts, axis=1)
            top = near_top[head, rows, :][:, :1]
            newest = jnp.maximum(top, jnp.max(scores, axis=1, keepdims=True))
            old = jnp.exp2(top - newest)
            weights = jnp.exp2(scores - newest)
            total = near_total[head, rows, :][:, :1] * old + jnp.sum(weights, axis=1, keepdims=True)
            summed = near_sum[head, rows, :] * old + dot(weights.astype(BF16), far_value[head])
            mixed.append((summed / total).astype(BF16))
        return jnp.concatenate(mixed, axis=1)

    def hop(way, chain, part, number):
        index = (way * 7 + (number if chain == 0 else 4 + number)) * PARTS + part
        return pltpu.make_async_remote_copy(
            src_ref=stage.at[index],
            dst_ref=ring.at[index],
            send_sem=ring_send.at[index],
            recv_sem=ring_recv.at[index],
            device_id={"head": up if way == 0 else down},
            device_id_type=MESH,
        ), index

    def columns_of(half, part):
        first = half * HALF + part * COLS
        return slice(first, first + COLS)

    def own(way, chain, part, distance):
        half = way if chain == 0 else 1 - way
        target = (z + distance) % RING if way == 0 else (z + RING - distance) % RING
        first = pl.multiple_of(target * PIECE, PIECE)
        return partial[pl.ds(first, PIECE), columns_of(half, part)]

    hops = []

    def send(way, chain, part, number):
        copy, index = hop(way, chain, part, number)
        term = own(way, chain, part, 4 - number if chain == 0 else 3 - number)
        if number > 0:
            before, previous = hop(way, chain, part, number - 1)
            before.wait_recv()
            term = term + ring[previous].astype(F32)
        stage[index] = term.astype(BF16)
        copy.start()
        hops.append(copy)

    load_out.wait()
    opposite = pl.ds(pl.multiple_of(((z + RING // 2) % RING) * PIECE, PIECE), PIECE)
    attention = attend(opposite)
    for part in range(PARTS):
        for way in range(2):
            copy, index = hop(way, 0, part, 0)
            stage[index] = dot(attention, wo[:, columns_of(way, part)]).astype(BF16)
            copy.start()
            hops.append(copy)

    partial[...] = dot(attend(slice(0, ROWS)), wo[...])
    for part in range(PARTS):
        for way in range(2):
            send(way, 1, part, 0)
    for number in range(1, 4):
        for chain in range(2):
            if chain == 1 and number == 3:
                continue
            for part in range(PARTS):
                for way in range(2):
                    send(way, chain, part, number)
    for copy in hops[:-4]:
        copy.wait_send()
    for level in range(1, LEVELS + 1):
        if level in FORWARD:
            handover(level).wait_send()
            pltpu.make_async_copy(received(level), received(level), send_sem.at[level - 1]).wait()
        else:
            pltpu.make_async_copy(lands[level - 1], lands[level - 1], send_sem.at[level - 1]).wait()
    mine = pl.ds(pl.multiple_of(z * PIECE, PIECE), PIECE)
    for half in range(2):
        short, index = hop(1 - half, 1, 0, 2)
        short.wait_recv()
        partial[mine, columns_of(half, 0)] += ring[index].astype(F32)
    for copy in hops[-4:-2]:
        copy.wait_send()
    for half in range(2):
        long, index = hop(half, 0, 0, 3)
        long.wait_recv()
        columns = columns_of(half, 0)
        out_ref[:, columns] = (partial[mine, columns] + ring[index].astype(F32)).astype(BF16)
    for copy in hops[-2:]:
        copy.wait_send()


def shards(tokens, w_query, w_key, w_value, w_out):
    message = [(2 * (ROWS >> level), WIDTH) for level in range(1, LEVELS + 1)]
    return pl.pallas_call(
        kernel,
        out_shape=jax.ShapeDtypeStruct((PIECE, MODEL), BF16),
        in_specs=[pl.BlockSpec(memory_space=pl.ANY)] * 5,
        out_specs=pl.BlockSpec(memory_space=pltpu.VMEM),
        scratch_shapes=[
            pltpu.VMEM((ROWS, MODEL), BF16),
            pltpu.VMEM((MODEL, WIDTH), BF16),
            pltpu.VMEM((MODEL, WIDTH), BF16),
            pltpu.VMEM((MODEL, WIDTH), BF16),
            pltpu.VMEM((WIDTH, MODEL), BF16),
            *[pltpu.VMEM(shape, BF16) for shape in message],
            *[pltpu.VMEM((1 << i, *shape), BF16) for i, shape in enumerate(message)],
            pltpu.VMEM((LEVELS, 2, ROWS, 2 * HEAD_DIM), BF16),
            pltpu.VMEM((2, ROWS, HEAD_DIM), F32),
            pltpu.VMEM((2, ROWS, HEAD_DIM), F32),
            pltpu.VMEM((2, ROWS, HEAD_DIM), F32),
            pltpu.VMEM((2, FAR, 2 * HEAD_DIM), BF16),
            pltpu.VMEM((2, FAR, HEAD_DIM), BF16),
            pltpu.VMEM((ROWS, MODEL), F32),
            pltpu.VMEM((14 * PARTS, PIECE, COLS), BF16),
            pltpu.VMEM((14 * PARTS, PIECE, COLS), BF16),
            pltpu.SemaphoreType.DMA((3 * CHUNKS + 2,)),
            pltpu.SemaphoreType.DMA((LEVELS,)),
            pltpu.SemaphoreType.DMA((LEVELS,)),
            pltpu.SemaphoreType.DMA((LEVELS,)),
            pltpu.SemaphoreType.DMA((LEVELS,)),
            pltpu.SemaphoreType.DMA((14 * PARTS,)),
            pltpu.SemaphoreType.DMA((14 * PARTS,)),
        ],
        compiler_params=pltpu.CompilerParams(
            collective_id=0, has_side_effects=True, vmem_limit_bytes=VMEM_BYTES
        ),
    )(tokens, w_query, w_key, w_value, w_out)


def solution(mesh):
    placed = (P("seq", None), P(None, "head"), P(None, "head"), P(None, "head"), P("head", None))
    return jax.shard_map(
        shards, mesh=mesh, in_specs=placed, out_specs=P(("seq", "head"), None), check_vma=False
    )
```

```python
import functools
import math

import jax
import jax.numpy as jnp
from jax import lax
from jax.experimental import pallas as pl
from jax.experimental.pallas import tpu as pltpu
from jax.sharding import PartitionSpec as P

HEAD_DIM = 128
ROWS = 256
WIDTH = 256
MODEL = 2048
HALF = MODEL // 2
PARTS = 1
COLS = HALF // PARTS
LEVELS = 5
FAR = LEVELS * HEAD_DIM
WEIGHTS = tuple(2.0**level for level in range(LEVELS + 1))
ORDER = (5, 4, 3, 2, 1)
FORWARD = (2, 3, 4, 5,)
CHUNKS = 4
DEPTH = MODEL // CHUNKS
SEQ = 32
RING = 8
PIECE = ROWS // RING
LOG2_E = 1.4426950408889634
SCORE_SCALE = LOG2_E / math.sqrt(HEAD_DIM)
MESH = pl.DeviceIdType.MESH
BF16 = jnp.bfloat16
F32 = jnp.float32
VMEM_BYTES = 107 * 512 * 1024


def dot(a, b):
    return jnp.dot(a, b, preferred_element_type=F32)


def dot_nt(a, b):
    return lax.dot_general(a, b, (((1,), (1,)), ((), ())), preferred_element_type=F32)


def averaging_rows(level):
    row = lax.broadcasted_iota(jnp.int32, (ROWS, ROWS), 0)
    col = lax.broadcasted_iota(jnp.int32, (ROWS, ROWS), 1)
    same = (row >> level) == (col >> level)
    return jnp.where(same, 2.0**-level, 0.0).astype(BF16)


def coarse_matrix():
    row = lax.broadcasted_iota(jnp.int32, (ROWS, ROWS), 0)
    col = lax.broadcasted_iota(jnp.int32, (ROWS, ROWS), 1)
    total = jnp.zeros((ROWS, ROWS), F32)
    start = 0
    for level in range(1, LEVELS + 1):
        count = ROWS >> level
        hit = (row >= start) & (row < start + count) & ((col >> level) == row - start)
        total = jnp.where(hit, 2.0**-level, total)
        start += count
    return total.astype(BF16)


def kernel(
    tok_hbm, wq_hbm, wk_hbm, wv_hbm, wo_hbm, out_ref,
    tok, wq, wk, wv, wo,
    send1, send2, send3, send4, send5,
    land1, land2, land3, land4, land5,
    fine, near_top, near_total, near_sum, far_key, far_value,
    partial, stage, ring,
    load_sem, send_sem, recv_sem, pass_send, pass_recv, ring_send, ring_recv,
):
    sends = (send1, send2, send3, send4, send5)
    lands = (land1, land2, land3, land4, land5)
    me = lax.axis_index("seq")
    z = lax.axis_index("head")
    core = me % 2

    barrier = pltpu.get_barrier_semaphore()

    up, down = (z + 1) % RING, (z + RING - 1) % RING
    for neighbour in (up, down):
        pl.semaphore_signal(barrier, inc=1, device_id={"head": neighbour}, device_id_type=MESH)

    def greet(step, carry):
        pl.semaphore_signal(
            barrier, inc=1, device_id={"seq": (me + 2 * step) % SEQ}, device_id_type=MESH
        )
        return carry

    lax.fori_loop(1, SEQ // 2, greet, 0)
    pl.semaphore_signal(barrier, inc=1, device_id={"seq": me ^ 1}, device_id_type=MESH)
    loads = []
    for c in range(CHUNKS):
        span = pl.ds(c * DEPTH, DEPTH)
        for src, dst in (
            (tok_hbm.at[:, span], tok.at[:, span]),
            (wk_hbm.at[span], wk.at[span]),
            (wv_hbm.at[span], wv.at[span]),
        ):
            loads.append(pltpu.make_async_copy(src, dst, load_sem.at[len(loads)]))
    load_query = pltpu.make_async_copy(wq_hbm, wq, load_sem.at[3 * CHUNKS])
    load_out = pltpu.make_async_copy(wo_hbm, wo, load_sem.at[3 * CHUNKS + 1])
    for load in (*loads, load_query, load_out):
        load.start()

    averages = coarse_matrix()
    acc_key = jnp.zeros((ROWS, WIDTH), F32)
    acc_value = jnp.zeros((ROWS, WIDTH), F32)
    for c in range(CHUNKS):
        for load in loads[3 * c:3 * c + 3]:
            load.wait()
        span = slice(c * DEPTH, (c + 1) * DEPTH)
        acc_key += dot(tok[:, span], wk[span, :])
        acc_value += dot(tok[:, span], wv[span, :])
    key = acc_key.astype(BF16)
    value = acc_value.astype(BF16)
    def coarsen(levels, start):
        rows = sum(ROWS >> level for level in levels)
        matrix = averages[start:start + rows]
        coarse_key = dot(matrix, key)
        coarse_value = dot(matrix, value)
        first = 0
        for level in levels:
            section = slice(first, first + (ROWS >> level))
            sends[level - 1][...] = jnp.concatenate(
                [coarse_key[section], coarse_value[section]], axis=0
            ).astype(BF16)
            first += ROWS >> level

    coarsen((2, 3, 4, 5), HEAD_DIM)
    pl.semaphore_wait(barrier, SEQ // 2 - 1 + 1 + 2)

    for level in ORDER:
        if level == 1:
            coarsen((1,), 0)
        many = 1 << (level - 1)
        first = ((me // many) ^ 1) * many
        place = me % many
        slot = place if level == 1 else core * (many // 2) + place // 2
        step_of = 2 if level in FORWARD else 1

        def post(step, carry, level=level, many=many, first=first, place=place, slot=slot, by=step_of):
            pltpu.make_async_remote_copy(
                src_ref=sends[level - 1],
                dst_ref=lands[level - 1].at[slot],
                send_sem=send_sem.at[level - 1],
                recv_sem=recv_sem.at[level - 1],
                device_id={"seq": first + (by * step + place) % many},
                device_id_type=MESH,
            ).start()
            return carry

        lax.fori_loop(0, many // step_of, post, 0)

    for level in range(1, LEVELS + 1):
        rows = slice((level - 1) * HEAD_DIM, level * HEAD_DIM)
        for head in range(2):
            far_value[head, rows, HEAD_DIM:] = jnp.full((HEAD_DIM, HEAD_DIM), WEIGHTS[level], BF16)

    load_query.wait()
    query = dot(tok[...], wq[...]).astype(BF16)
    for level in range(1, LEVELS + 1):
        wide = dot(averaging_rows(level), query) * SCORE_SCALE
        high = wide.astype(BF16)
        low = (wide - high.astype(F32)).astype(BF16)
        for head in range(2):
            cols = slice(head * HEAD_DIM, (head + 1) * HEAD_DIM)
            fine[level - 1, head, :, :HEAD_DIM] = high[:, cols]
            fine[level - 1, head, :, HEAD_DIM:] = low[:, cols]

    for head in range(2):
        cols = slice(head * HEAD_DIM, (head + 1) * HEAD_DIM)
        scores = dot_nt(query[:, cols], key[:, cols]) * SCORE_SCALE
        top = jnp.max(scores, axis=1, keepdims=True)
        weights = jnp.exp2(scores - top)
        total = jnp.sum(weights, axis=1, keepdims=True)
        near_top[head] = jnp.broadcast_to(top, (ROWS, HEAD_DIM))
        near_total[head] = jnp.broadcast_to(total, (ROWS, HEAD_DIM))
        near_sum[head] = dot(weights.astype(BF16), value[:, cols])

    def received(level):
        return lands[level - 1].at[pl.ds(core * (1 << (level - 2)), 1 << (level - 2))]

    def passed(level):
        return lands[level - 1].at[pl.ds((1 - core) * (1 << (level - 2)), 1 << (level - 2))]

    def handover(level):
        return pltpu.make_async_remote_copy(
            src_ref=received(level),
            dst_ref=received(level),
            send_sem=pass_send.at[level - 1],
            recv_sem=pass_recv.at[level - 1],
            device_id={"seq": me ^ 1},
            device_id_type=MESH,
        )

    def take(level, slots, place):
        count = ROWS >> level
        block = lands[level - 1][slots]
        if count < 16:
            block = block.astype(F32)
        length = block.shape[0] * count
        keys = block[:, :count, :].reshape(length, WIDTH).astype(BF16)
        values = block[:, count:, :].reshape(length, WIDTH).astype(BF16)
        rows = slice((level - 1) * HEAD_DIM + place, (level - 1) * HEAD_DIM + place + length)
        for head in range(2):
            cols = slice(head * HEAD_DIM, (head + 1) * HEAD_DIM)
            far_key[head, rows, :HEAD_DIM] = keys[:, cols]
            far_key[head, rows, HEAD_DIM:] = keys[:, cols]
            far_value[head, rows, :HEAD_DIM] = values[:, cols] * WEIGHTS[level]

    for level in (4, 5, 3, 2):
        pltpu.make_async_copy(received(level), received(level), recv_sem.at[level - 1]).wait()
        handover(level).start()
    pltpu.make_async_copy(land1, land1, recv_sem.at[0]).wait()
    take(1, slice(0, 1), 0)
    for level in FORWARD:
        take(level, pl.ds(core * (1 << (level - 2)), 1 << (level - 2)), 0)
    for level in (4, 5, 3, 2):
        pltpu.make_async_copy(passed(level), passed(level), pass_recv.at[level - 1]).wait()
        take(level, pl.ds((1 - core) * (1 << (level - 2)), 1 << (level - 2)), HEAD_DIM // 2)

    def attend(rows):
        mixed = []
        for head in range(2):
            parts = []
            for level in range(1, LEVELS + 1):
                section = slice((level - 1) * HEAD_DIM, level * HEAD_DIM)
                parts.append(dot_nt(fine[level - 1, head, rows, :], far_key[head, section, :]))
            highest = functools.reduce(jnp.maximum, parts)
            top = near_top[head, rows, :]
            newest = jnp.maximum(top, jnp.max(highest, axis=1, keepdims=True) + float(LEVELS))
            old = jnp.exp2(top - newest)
            weights = jnp.concatenate([jnp.exp2(part - newest).astype(BF16) for part in parts], axis=1)
            far = dot(weights, far_value[head])
            summed = near_sum[head, rows, :] * old + far[:, :HEAD_DIM]
            total = near_total[head, rows, :] * old + far[:, HEAD_DIM:]
            mixed.append((summed / total).astype(BF16))
        return jnp.concatenate(mixed, axis=1)

    def hop(way, chain, part, number):
        index = (way * 7 + (number if chain == 0 else 4 + number)) * PARTS + part
        return pltpu.make_async_remote_copy(
            src_ref=stage.at[index],
            dst_ref=ring.at[index],
            send_sem=ring_send.at[index],
            recv_sem=ring_recv.at[index],
            device_id={"head": up if way == 0 else down},
            device_id_type=MESH,
        ), index

    def columns_of(half, part):
        first = half * HALF + part * COLS
        return slice(first, first + COLS)

    def own(way, chain, part, distance):
        half = way if chain == 0 else 1 - way
        target = (z + distance) % RING if way == 0 else (z + RING - distance) % RING
        first = pl.multiple_of(target * PIECE, PIECE)
        return partial[pl.ds(first, PIECE), columns_of(half, part)]

    hops = []

    def send(way, chain, part, number):
        copy, index = hop(way, chain, part, number)
        term = own(way, chain, part, 4 - number if chain == 0 else 3 - number)
        if number > 0:
            before, previous = hop(way, chain, part, number - 1)
            before.wait_recv()
            term = term + ring[previous].astype(F32)
        stage[index] = term.astype(BF16)
        copy.start()
        hops.append(copy)

    load_out.wait()
    opposite = pl.ds(pl.multiple_of(((z + RING // 2) % RING) * PIECE, PIECE), PIECE)
    attention = attend(opposite)
    for part in range(PARTS):
        for way in range(2):
            copy, index = hop(way, 0, part, 0)
            stage[index] = dot(attention, wo[:, columns_of(way, part)]).astype(BF16)
            copy.start()
            hops.append(copy)

    partial[...] = dot(attend(slice(0, ROWS)), wo[...])
    for part in range(PARTS):
        for way in range(2):
            send(way, 1, part, 0)
    for number in range(1, 4):
        for chain in range(2):
            if chain == 1 and number == 3:
                continue
            for part in range(PARTS):
                for way in range(2):
                    send(way, chain, part, number)
    for copy in hops[:-4]:
        copy.wait_send()
    for level in range(1, LEVELS + 1):
        if level in FORWARD:
            handover(level).wait_send()
            pltpu.make_async_copy(received(level), received(level), send_sem.at[level - 1]).wait()
        else:
            pltpu.make_async_copy(lands[level - 1], lands[level - 1], send_sem.at[level - 1]).wait()
    mine = pl.ds(pl.multiple_of(z * PIECE, PIECE), PIECE)
    for half in range(2):
        short, index = hop(1 - half, 1, 0, 2)
        short.wait_recv()
        partial[mine, columns_of(half, 0)] += ring[index].astype(F32)
    for copy in hops[-4:-2]:
        copy.wait_send()
    for half in range(2):
        long, index = hop(half, 0, 0, 3)
        long.wait_recv()
        columns = columns_of(half, 0)
        out_ref[:, columns] = (partial[mine, columns] + ring[index].astype(F32)).astype(BF16)
    for copy in hops[-2:]:
        copy.wait_send()


def shards(tokens, w_query, w_key, w_value, w_out):
    message = [(2 * (ROWS >> level), WIDTH) for level in range(1, LEVELS + 1)]
    return pl.pallas_call(
        kernel,
        out_shape=jax.ShapeDtypeStruct((PIECE, MODEL), BF16),
        in_specs=[pl.BlockSpec(memory_space=pl.ANY)] * 5,
        out_specs=pl.BlockSpec(memory_space=pltpu.VMEM),
        scratch_shapes=[
            pltpu.VMEM((ROWS, MODEL), BF16),
            pltpu.VMEM((MODEL, WIDTH), BF16),
            pltpu.VMEM((MODEL, WIDTH), BF16),
            pltpu.VMEM((MODEL, WIDTH), BF16),
            pltpu.VMEM((WIDTH, MODEL), BF16),
            *[pltpu.VMEM(shape, BF16) for shape in message],
            *[pltpu.VMEM((1 << i, *shape), BF16) for i, shape in enumerate(message)],
            pltpu.VMEM((LEVELS, 2, ROWS, 2 * HEAD_DIM), BF16),
            pltpu.VMEM((2, ROWS, HEAD_DIM), F32),
            pltpu.VMEM((2, ROWS, HEAD_DIM), F32),
            pltpu.VMEM((2, ROWS, HEAD_DIM), F32),
            pltpu.VMEM((2, FAR, 2 * HEAD_DIM), BF16),
            pltpu.VMEM((2, FAR, 2 * HEAD_DIM), BF16),
            pltpu.VMEM((ROWS, MODEL), F32),
            pltpu.VMEM((14 * PARTS, PIECE, COLS), BF16),
            pltpu.VMEM((14 * PARTS, PIECE, COLS), BF16),
            pltpu.SemaphoreType.DMA((3 * CHUNKS + 2,)),
            pltpu.SemaphoreType.DMA((LEVELS,)),
            pltpu.SemaphoreType.DMA((LEVELS,)),
            pltpu.SemaphoreType.DMA((LEVELS,)),
            pltpu.SemaphoreType.DMA((LEVELS,)),
            pltpu.SemaphoreType.DMA((14 * PARTS,)),
            pltpu.SemaphoreType.DMA((14 * PARTS,)),
        ],
        compiler_params=pltpu.CompilerParams(
            collective_id=0, has_side_effects=True, vmem_limit_bytes=VMEM_BYTES
        ),
    )(tokens, w_query, w_key, w_value, w_out)


def solution(mesh):
    placed = (P("seq", None), P(None, "head"), P(None, "head"), P(None, "head"), P("head", None))
    return jax.shard_map(
        shards, mesh=mesh, in_specs=placed, out_specs=P(("seq", "head"), None), check_vma=False
    )
```

```python
import functools
import math

import jax
import jax.numpy as jnp
from jax import lax
from jax.experimental import pallas as pl
from jax.experimental.pallas import tpu as pltpu
from jax.sharding import PartitionSpec as P

HEAD_DIM = 128
ROWS = 256
WIDTH = 256
MODEL = 2048
HALF = MODEL // 2
PARTS = 1
COLS = HALF // PARTS
LEVELS = 5
FAR = LEVELS * HEAD_DIM
ORDER = (5, 4, 3, 2, 1)
FORWARD = (2, 3, 4, 5,)
CHUNKS = 4
DEPTH = MODEL // CHUNKS
SEQ = 32
RING = 8
PIECE = ROWS // RING
LOG2_E = 1.4426950408889634
SCORE_SCALE = LOG2_E / math.sqrt(HEAD_DIM)
MESH = pl.DeviceIdType.MESH
BF16 = jnp.bfloat16
F32 = jnp.float32
VMEM_BYTES = 107 * 512 * 1024


def dot(a, b):
    return jnp.dot(a, b, preferred_element_type=F32)


def dot_nt(a, b):
    return lax.dot_general(a, b, (((1,), (1,)), ((), ())), preferred_element_type=F32)


def averaging_rows(level):
    row = lax.broadcasted_iota(jnp.int32, (ROWS, ROWS), 0)
    col = lax.broadcasted_iota(jnp.int32, (ROWS, ROWS), 1)
    same = (row >> level) == (col >> level)
    return jnp.where(same, 2.0**-level, 0.0).astype(BF16)


def coarse_matrix():
    row = lax.broadcasted_iota(jnp.int32, (ROWS, ROWS), 0)
    col = lax.broadcasted_iota(jnp.int32, (ROWS, ROWS), 1)
    total = jnp.zeros((ROWS, ROWS), F32)
    start = 0
    for level in range(1, LEVELS + 1):
        count = ROWS >> level
        hit = (row >= start) & (row < start + count) & ((col >> level) == row - start)
        total = jnp.where(hit, 2.0**-level, total)
        start += count
    return total.astype(BF16)


def kernel(
    tok_hbm, wq_hbm, wk_hbm, wv_hbm, wo_hbm, out_ref,
    tok, wq, wk, wv, wo,
    send1, send2, send3, send4, send5,
    land1, land2, land3, land4, land5,
    fine, near_top, near_total, near_sum, far_key, far_value,
    partial, stage, ring,
    load_sem, send_sem, recv_sem, pass_send, pass_recv, ring_send, ring_recv,
):
    sends = (send1, send2, send3, send4, send5)
    lands = (land1, land2, land3, land4, land5)
    me = lax.axis_index("seq")
    z = lax.axis_index("head")
    core = me % 2

    barrier = pltpu.get_barrier_semaphore()

    up, down = (z + 1) % RING, (z + RING - 1) % RING
    for neighbour in (up, down):
        pl.semaphore_signal(barrier, inc=1, device_id={"head": neighbour}, device_id_type=MESH)

    def greet(step, carry):
        pl.semaphore_signal(
            barrier, inc=1, device_id={"seq": (me + 2 * step) % SEQ}, device_id_type=MESH
        )
        return carry

    lax.fori_loop(1, SEQ // 2, greet, 0)
    pl.semaphore_signal(barrier, inc=1, device_id={"seq": me ^ 1}, device_id_type=MESH)
    loads = []
    for c in range(CHUNKS):
        span = pl.ds(c * DEPTH, DEPTH)
        for src, dst in (
            (tok_hbm.at[:, span], tok.at[:, span]),
            (wk_hbm.at[span], wk.at[span]),
            (wv_hbm.at[span], wv.at[span]),
        ):
            loads.append(pltpu.make_async_copy(src, dst, load_sem.at[len(loads)]))
    load_query = pltpu.make_async_copy(wq_hbm, wq, load_sem.at[3 * CHUNKS])
    load_out = pltpu.make_async_copy(wo_hbm, wo, load_sem.at[3 * CHUNKS + 1])
    for load in (*loads, load_query, load_out):
        load.start()

    averages = coarse_matrix()
    acc_key = jnp.zeros((ROWS, WIDTH), F32)
    acc_value = jnp.zeros((ROWS, WIDTH), F32)
    for c in range(CHUNKS):
        for load in loads[3 * c:3 * c + 3]:
            load.wait()
        span = slice(c * DEPTH, (c + 1) * DEPTH)
        acc_key += dot(tok[:, span], wk[span, :])
        acc_value += dot(tok[:, span], wv[span, :])
    key = acc_key.astype(BF16)
    value = acc_value.astype(BF16)
    coarse_key = dot(averages, key)
    coarse_value = dot(averages, value)
    start = 0
    for level in range(1, LEVELS + 1):
        count = ROWS >> level
        rows = slice(start, start + count)
        sends[level - 1][...] = jnp.concatenate(
            [coarse_key[rows], coarse_value[rows]], axis=0
        ).astype(BF16)
        start += count

    pl.semaphore_wait(barrier, SEQ // 2 - 1 + 1 + 2)

    for level in ORDER:
        many = 1 << (level - 1)
        first = ((me // many) ^ 1) * many
        place = me % many
        slot = place if level == 1 else core * (many // 2) + place // 2
        step_of = 2 if level in FORWARD else 1

        def post(step, carry, level=level, many=many, first=first, place=place, slot=slot, by=step_of):
            pltpu.make_async_remote_copy(
                src_ref=sends[level - 1],
                dst_ref=lands[level - 1].at[slot],
                send_sem=send_sem.at[level - 1],
                recv_sem=recv_sem.at[level - 1],
                device_id={"seq": first + (by * step + place) % many},
                device_id_type=MESH,
            ).start()
            return carry

        lax.fori_loop(0, many // step_of, post, 0)

    load_query.wait()
    query = dot(tok[...], wq[...]).astype(BF16)
    for level in range(1, LEVELS + 1):
        wide = dot(averaging_rows(level), query)
        high = wide.astype(BF16)
        low = (wide - high.astype(F32)).astype(BF16)
        for head in range(2):
            cols = slice(head * HEAD_DIM, (head + 1) * HEAD_DIM)
            fine[level - 1, head, :, :HEAD_DIM] = high[:, cols]
            fine[level - 1, head, :, HEAD_DIM:] = low[:, cols]

    for head in range(2):
        cols = slice(head * HEAD_DIM, (head + 1) * HEAD_DIM)
        scores = dot_nt(query[:, cols], key[:, cols]) * SCORE_SCALE
        top = jnp.max(scores, axis=1, keepdims=True)
        weights = jnp.exp2(scores - top)
        total = jnp.sum(weights, axis=1, keepdims=True)
        near_top[head] = jnp.broadcast_to(top, (ROWS, HEAD_DIM))
        near_total[head] = jnp.broadcast_to(total, (ROWS, HEAD_DIM))
        near_sum[head] = dot(weights.astype(BF16), value[:, cols])

    def received(level):
        return lands[level - 1].at[pl.ds(core * (1 << (level - 2)), 1 << (level - 2))]

    def passed(level):
        return lands[level - 1].at[pl.ds((1 - core) * (1 << (level - 2)), 1 << (level - 2))]

    def handover(level):
        return pltpu.make_async_remote_copy(
            src_ref=received(level),
            dst_ref=received(level),
            send_sem=pass_send.at[level - 1],
            recv_sem=pass_recv.at[level - 1],
            device_id={"seq": me ^ 1},
            device_id_type=MESH,
        )

    def take(level, slots, place):
        count = ROWS >> level
        block = lands[level - 1][slots]
        if count < 16:
            block = block.astype(F32)
        length = block.shape[0] * count
        keys = block[:, :count, :].reshape(length, WIDTH).astype(BF16)
        values = block[:, count:, :].reshape(length, WIDTH).astype(BF16)
        rows = slice((level - 1) * HEAD_DIM + place, (level - 1) * HEAD_DIM + place + length)
        for head in range(2):
            cols = slice(head * HEAD_DIM, (head + 1) * HEAD_DIM)
            far_key[head, rows, :HEAD_DIM] = keys[:, cols]
            far_key[head, rows, HEAD_DIM:] = keys[:, cols]
            far_value[head, rows, :] = values[:, cols]

    for level in (4, 5, 3, 2):
        pltpu.make_async_copy(received(level), received(level), recv_sem.at[level - 1]).wait()
        handover(level).start()
    pltpu.make_async_copy(land1, land1, recv_sem.at[0]).wait()
    take(1, slice(0, 1), 0)
    for level in FORWARD:
        take(level, pl.ds(core * (1 << (level - 2)), 1 << (level - 2)), 0)
    for level in (4, 5, 3, 2):
        pltpu.make_async_copy(passed(level), passed(level), pass_recv.at[level - 1]).wait()
        take(level, pl.ds((1 - core) * (1 << (level - 2)), 1 << (level - 2)), HEAD_DIM // 2)

    def attend(rows):
        mixed = []
        for head in range(2):
            parts = []
            for level in range(1, LEVELS + 1):
                section = slice((level - 1) * HEAD_DIM, level * HEAD_DIM)
                product = dot_nt(fine[level - 1, head, rows, :], far_key[head, section, :])
                parts.append(product * SCORE_SCALE + float(level))
            scores = jnp.concatenate(parts, axis=1)
            top = near_top[head, rows, :][:, :1]
            newest = jnp.maximum(top, jnp.max(scores, axis=1, keepdims=True))
            old = jnp.exp2(top - newest)
            weights = jnp.exp2(scores - newest)
            total = near_total[head, rows, :][:, :1] * old + jnp.sum(weights, axis=1, keepdims=True)
            summed = near_sum[head, rows, :] * old + dot(weights.astype(BF16), far_value[head])
            mixed.append((summed / total).astype(BF16))
        return jnp.concatenate(mixed, axis=1)

    def hop(way, chain, part, number):
        index = (way * 7 + (number if chain == 0 else 4 + number)) * PARTS + part
        return pltpu.make_async_remote_copy(
            src_ref=stage.at[index],
            dst_ref=ring.at[index],
            send_sem=ring_send.at[index],
            recv_sem=ring_recv.at[index],
            device_id={"head": up if way == 0 else down},
            device_id_type=MESH,
        ), index

    def columns_of(half, part):
        first = half * HALF + part * COLS
        return slice(first, first + COLS)

    def own(way, chain, part, distance):
        half = way if chain == 0 else 1 - way
        target = (z + distance) % RING if way == 0 else (z + RING - distance) % RING
        first = pl.multiple_of(target * PIECE, PIECE)
        return partial[pl.ds(first, PIECE), columns_of(half, part)]

    hops = []

    def send(way, chain, part, number):
        copy, index = hop(way, chain, part, number)
        term = own(way, chain, part, 4 - number if chain == 0 else 3 - number)
        if number > 0:
            before, previous = hop(way, chain, part, number - 1)
            before.wait_recv()
            term = term + ring[previous].astype(F32)
        stage[index] = term.astype(BF16)
        copy.start()
        hops.append(copy)

    load_out.wait()
    opposite = pl.ds(pl.multiple_of(((z + RING // 2) % RING) * PIECE, PIECE), PIECE)
    attention = attend(opposite)
    for part in range(PARTS):
        for way in range(2):
            copy, index = hop(way, 0, part, 0)
            stage[index] = dot(attention, wo[:, columns_of(way, part)]).astype(BF16)
            copy.start()
            hops.append(copy)

    partial[...] = dot(attend(slice(0, ROWS)), wo[...])
    for part in range(PARTS):
        for way in range(2):
            send(way, 1, part, 0)
    for number in range(1, 4):
        for chain in range(2):
            if chain == 1 and number == 3:
                continue
            for part in range(PARTS):
                for way in range(2):
                    send(way, chain, part, number)
    for copy in hops[:-4]:
        copy.wait_send()
    for level in range(1, LEVELS + 1):
        if level in FORWARD:
            handover(level).wait_send()
            pltpu.make_async_copy(received(level), received(level), send_sem.at[level - 1]).wait()
        else:
            pltpu.make_async_copy(lands[level - 1], lands[level - 1], send_sem.at[level - 1]).wait()
    mine = pl.ds(pl.multiple_of(z * PIECE, PIECE), PIECE)
    for half in range(2):
        short, index = hop(1 - half, 1, 0, 2)
        short.wait_recv()
        partial[mine, columns_of(half, 0)] += ring[index].astype(F32)
    for copy in hops[-4:-2]:
        copy.wait_send()
    for half in (1, 0):
        long, index = hop(half, 0, 0, 3)
        long.wait_recv()
        columns = columns_of(half, 0)
        out_ref[:, columns] = (partial[mine, columns] + ring[index].astype(F32)).astype(BF16)
    for copy in hops[-2:]:
        copy.wait_send()


def shards(tokens, w_query, w_key, w_value, w_out):
    message = [(2 * (ROWS >> level), WIDTH) for level in range(1, LEVELS + 1)]
    return pl.pallas_call(
        kernel,
        out_shape=jax.ShapeDtypeStruct((PIECE, MODEL), BF16),
        in_specs=[pl.BlockSpec(memory_space=pl.ANY)] * 5,
        out_specs=pl.BlockSpec(memory_space=pltpu.VMEM),
        scratch_shapes=[
            pltpu.VMEM((ROWS, MODEL), BF16),
            pltpu.VMEM((MODEL, WIDTH), BF16),
            pltpu.VMEM((MODEL, WIDTH), BF16),
            pltpu.VMEM((MODEL, WIDTH), BF16),
            pltpu.VMEM((WIDTH, MODEL), BF16),
            *[pltpu.VMEM(shape, BF16) for shape in message],
            *[pltpu.VMEM((1 << i, *shape), BF16) for i, shape in enumerate(message)],
            pltpu.VMEM((LEVELS, 2, ROWS, 2 * HEAD_DIM), BF16),
            pltpu.VMEM((2, ROWS, HEAD_DIM), F32),
            pltpu.VMEM((2, ROWS, HEAD_DIM), F32),
            pltpu.VMEM((2, ROWS, HEAD_DIM), F32),
            pltpu.VMEM((2, FAR, 2 * HEAD_DIM), BF16),
            pltpu.VMEM((2, FAR, HEAD_DIM), BF16),
            pltpu.VMEM((ROWS, MODEL), F32),
            pltpu.VMEM((14 * PARTS, PIECE, COLS), BF16),
            pltpu.VMEM((14 * PARTS, PIECE, COLS), BF16),
            pltpu.SemaphoreType.DMA((3 * CHUNKS + 2,)),
            pltpu.SemaphoreType.DMA((LEVELS,)),
            pltpu.SemaphoreType.DMA((LEVELS,)),
            pltpu.SemaphoreType.DMA((LEVELS,)),
            pltpu.SemaphoreType.DMA((LEVELS,)),
            pltpu.SemaphoreType.DMA((14 * PARTS,)),
            pltpu.SemaphoreType.DMA((14 * PARTS,)),
        ],
        compiler_params=pltpu.CompilerParams(
            collective_id=0, has_side_effects=True, vmem_limit_bytes=VMEM_BYTES
        ),
    )(tokens, w_query, w_key, w_value, w_out)


def solution(mesh):
    placed = (P("seq", None), P(None, "head"), P(None, "head"), P(None, "head"), P("head", None))
    return jax.shard_map(
        shards, mesh=mesh, in_specs=placed, out_specs=P(("seq", "head"), None), check_vma=False
    )
```

```python
import functools
import math

import jax
import jax.numpy as jnp
from jax import lax
from jax.experimental import pallas as pl
from jax.experimental.pallas import tpu as pltpu
from jax.sharding import PartitionSpec as P

HEAD_DIM = 128
ROWS = 256
WIDTH = 256
MODEL = 2048
HALF = MODEL // 2
PARTS = 1
COLS = HALF // PARTS
LEVELS = 5
FAR = LEVELS * HEAD_DIM
ORDER = (5, 4, 3, 2, 1)
FORWARD = (2, 3, 4, 5,)
CHUNKS = 4
DEPTH = MODEL // CHUNKS
SEQ = 32
RING = 8
PIECE = ROWS // RING
LOG2_E = 1.4426950408889634
SCORE_SCALE = LOG2_E / math.sqrt(HEAD_DIM)
MESH = pl.DeviceIdType.MESH
BF16 = jnp.bfloat16
F32 = jnp.float32
VMEM_BYTES = 107 * 512 * 1024


def dot(a, b):
    return jnp.dot(a, b, preferred_element_type=F32)


def dot_nt(a, b):
    return lax.dot_general(a, b, (((1,), (1,)), ((), ())), preferred_element_type=F32)


def averaging_rows(level):
    row = lax.broadcasted_iota(jnp.int32, (ROWS, ROWS), 0)
    col = lax.broadcasted_iota(jnp.int32, (ROWS, ROWS), 1)
    same = (row >> level) == (col >> level)
    return jnp.where(same, 2.0**-level, 0.0).astype(BF16)


def coarse_matrix():
    row = lax.broadcasted_iota(jnp.int32, (ROWS, ROWS), 0)
    col = lax.broadcasted_iota(jnp.int32, (ROWS, ROWS), 1)
    total = jnp.zeros((ROWS, ROWS), F32)
    start = 0
    for level in range(1, LEVELS + 1):
        count = ROWS >> level
        hit = (row >= start) & (row < start + count) & ((col >> level) == row - start)
        total = jnp.where(hit, 2.0**-level, total)
        start += count
    return total.astype(BF16)


def kernel(
    tok_hbm, wq_hbm, wk_hbm, wv_hbm, wo_hbm, out_ref,
    tok, wq, wk, wv, wo,
    send1, send2, send3, send4, send5,
    land1, land2, land3, land4, land5,
    fine, near_top, near_total, near_sum, far_key, far_value,
    partial, stage, ring,
    load_sem, send_sem, recv_sem, pass_send, pass_recv, ring_send, ring_recv,
):
    sends = (send1, send2, send3, send4, send5)
    lands = (land1, land2, land3, land4, land5)
    me = lax.axis_index("seq")
    z = lax.axis_index("head")
    core = me % 2

    barrier = pltpu.get_barrier_semaphore()

    def greet(step, carry):
        pl.semaphore_signal(
            barrier, inc=1, device_id={"seq": (me + 2 * step) % SEQ}, device_id_type=MESH
        )
        return carry

    lax.fori_loop(1, SEQ // 2, greet, 0)
    pl.semaphore_signal(barrier, inc=1, device_id={"seq": me ^ 1}, device_id_type=MESH)
    up, down = (z + 1) % RING, (z + RING - 1) % RING
    for neighbour in (up, down):
        pl.semaphore_signal(barrier, inc=1, device_id={"head": neighbour}, device_id_type=MESH)

    loads = []
    for c in range(CHUNKS):
        span = pl.ds(c * DEPTH, DEPTH)
        for src, dst in (
            (tok_hbm.at[:, span], tok.at[:, span]),
            (wk_hbm.at[span], wk.at[span]),
            (wv_hbm.at[span], wv.at[span]),
        ):
            loads.append(pltpu.make_async_copy(src, dst, load_sem.at[len(loads)]))
    load_query = pltpu.make_async_copy(wq_hbm, wq, load_sem.at[3 * CHUNKS])
    load_out = pltpu.make_async_copy(wo_hbm, wo, load_sem.at[3 * CHUNKS + 1])
    for load in (*loads, load_query, load_out):
        load.start()

    averages = coarse_matrix()
    acc_key = jnp.zeros((ROWS, WIDTH), F32)
    acc_value = jnp.zeros((ROWS, WIDTH), F32)
    for c in range(CHUNKS):
        for load in loads[3 * c:3 * c + 3]:
            load.wait()
        span = slice(c * DEPTH, (c + 1) * DEPTH)
        acc_key += dot(tok[:, span], wk[span, :])
        acc_value += dot(tok[:, span], wv[span, :])
    key = acc_key.astype(BF16)
    value = acc_value.astype(BF16)
    coarse_key = dot(averages, key)
    coarse_value = dot(averages, value)
    start = 0
    for level in range(1, LEVELS + 1):
        count = ROWS >> level
        rows = slice(start, start + count)
        sends[level - 1][...] = jnp.concatenate(
            [coarse_key[rows], coarse_value[rows]], axis=0
        ).astype(BF16)
        start += count

    pl.semaphore_wait(barrier, SEQ // 2 - 1 + 1 + 2)

    for level in ORDER:
        many = 1 << (level - 1)
        first = ((me // many) ^ 1) * many
        place = me % many
        slot = place if level == 1 else core * (many // 2) + place // 2
        step_of = 2 if level in FORWARD else 1

        def post(step, carry, level=level, many=many, first=first, place=place, slot=slot, by=step_of):
            pltpu.make_async_remote_copy(
                src_ref=sends[level - 1],
                dst_ref=lands[level - 1].at[slot],
                send_sem=send_sem.at[level - 1],
                recv_sem=recv_sem.at[level - 1],
                device_id={"seq": first + (by * step + place) % many},
                device_id_type=MESH,
            ).start()
            return carry

        lax.fori_loop(0, many // step_of, post, 0)

    load_query.wait()
    query = dot(tok[...], wq[...]).astype(BF16)
    for level in range(1, LEVELS + 1):
        wide = dot(averaging_rows(level), query)
        high = wide.astype(BF16)
        low = (wide - high.astype(F32)).astype(BF16)
        for head in range(2):
            cols = slice(head * HEAD_DIM, (head + 1) * HEAD_DIM)
            fine[level - 1, head, :, :HEAD_DIM] = high[:, cols]
            fine[level - 1, head, :, HEAD_DIM:] = low[:, cols]

    for head in range(2):
        cols = slice(head * HEAD_DIM, (head + 1) * HEAD_DIM)
        scores = dot_nt(query[:, cols], key[:, cols]) * SCORE_SCALE
        top = jnp.max(scores, axis=1, keepdims=True)
        weights = jnp.exp2(scores - top)
        total = jnp.sum(weights, axis=1, keepdims=True)
        near_top[head] = jnp.broadcast_to(top, (ROWS, HEAD_DIM))
        near_total[head] = jnp.broadcast_to(total, (ROWS, HEAD_DIM))
        near_sum[head] = dot(weights.astype(BF16), value[:, cols])

    def received(level):
        return lands[level - 1].at[pl.ds(core * (1 << (level - 2)), 1 << (level - 2))]

    def passed(level):
        return lands[level - 1].at[pl.ds((1 - core) * (1 << (level - 2)), 1 << (level - 2))]

    def handover(level):
        return pltpu.make_async_remote_copy(
            src_ref=received(level),
            dst_ref=received(level),
            send_sem=pass_send.at[level - 1],
            recv_sem=pass_recv.at[level - 1],
            device_id={"seq": me ^ 1},
            device_id_type=MESH,
        )

    def take(level, slots, place):
        count = ROWS >> level
        block = lands[level - 1][slots]
        if count < 16:
            block = block.astype(F32)
        length = block.shape[0] * count
        keys = block[:, :count, :].reshape(length, WIDTH).astype(BF16)
        values = block[:, count:, :].reshape(length, WIDTH).astype(BF16)
        rows = slice((level - 1) * HEAD_DIM + place, (level - 1) * HEAD_DIM + place + length)
        for head in range(2):
            cols = slice(head * HEAD_DIM, (head + 1) * HEAD_DIM)
            far_key[head, rows, :HEAD_DIM] = keys[:, cols]
            far_key[head, rows, HEAD_DIM:] = keys[:, cols]
            far_value[head, rows, :] = values[:, cols]

    for level in (4, 5, 3, 2):
        pltpu.make_async_copy(received(level), received(level), recv_sem.at[level - 1]).wait()
        handover(level).start()
    pltpu.make_async_copy(land1, land1, recv_sem.at[0]).wait()
    take(1, slice(0, 1), 0)
    for level in FORWARD:
        take(level, pl.ds(core * (1 << (level - 2)), 1 << (level - 2)), 0)
    for level in (4, 5, 3, 2):
        pltpu.make_async_copy(passed(level), passed(level), pass_recv.at[level - 1]).wait()
        take(level, pl.ds((1 - core) * (1 << (level - 2)), 1 << (level - 2)), HEAD_DIM // 2)

    def attend(rows):
        mixed = []
        for head in range(2):
            parts = []
            for level in range(1, LEVELS + 1):
                section = slice((level - 1) * HEAD_DIM, level * HEAD_DIM)
                product = dot_nt(fine[level - 1, head, rows, :], far_key[head, section, :])
                parts.append(product * SCORE_SCALE + float(level))
            scores = jnp.concatenate(parts, axis=1)
            top = near_top[head, rows, :][:, :1]
            newest = jnp.maximum(top, jnp.max(scores, axis=1, keepdims=True))
            old = jnp.exp2(top - newest)
            weights = jnp.exp2(scores - newest)
            total = near_total[head, rows, :][:, :1] * old + jnp.sum(weights, axis=1, keepdims=True)
            summed = near_sum[head, rows, :] * old + dot(weights.astype(BF16), far_value[head])
            mixed.append((summed / total).astype(BF16))
        return jnp.concatenate(mixed, axis=1)

    def hop(way, chain, part, number):
        index = (way * 7 + (number if chain == 0 else 4 + number)) * PARTS + part
        return pltpu.make_async_remote_copy(
            src_ref=stage.at[index],
            dst_ref=ring.at[index],
            send_sem=ring_send.at[index],
            recv_sem=ring_recv.at[index],
            device_id={"head": up if way == 0 else down},
            device_id_type=MESH,
        ), index

    def columns_of(half, part):
        first = half * HALF + part * COLS
        return slice(first, first + COLS)

    def own(way, chain, part, distance):
        half = way if chain == 0 else 1 - way
        target = (z + distance) % RING if way == 0 else (z + RING - distance) % RING
        first = pl.multiple_of(target * PIECE, PIECE)
        return partial[pl.ds(first, PIECE), columns_of(half, part)]

    hops = []

    def send(way, chain, part, number):
        copy, index = hop(way, chain, part, number)
        term = own(way, chain, part, 4 - number if chain == 0 else 3 - number)
        if number > 0:
            before, previous = hop(way, chain, part, number - 1)
            before.wait_recv()
            term = term + ring[previous].astype(F32)
        stage[index] = term.astype(BF16)
        copy.start()
        hops.append(copy)

    load_out.wait()
    opposite = pl.ds(pl.multiple_of(((z + RING // 2) % RING) * PIECE, PIECE), PIECE)
    attention = attend(opposite)
    for part in range(PARTS):
        for way in range(2):
            copy, index = hop(way, 0, part, 0)
            stage[index] = dot(attention, wo[:, columns_of(way, part)]).astype(BF16)
            copy.start()
            hops.append(copy)

    partial[...] = dot(attend(slice(0, ROWS)), wo[...])
    for part in range(PARTS):
        for way in (1, 0):
            send(way, 1, part, 0)
    for number in range(1, 4):
        for chain in range(2):
            if chain == 1 and number == 3:
                continue
            for part in range(PARTS):
                for way in range(2):
                    send(way, chain, part, number)
    for copy in hops[:-4]:
        copy.wait_send()
    for level in range(1, LEVELS + 1):
        if level in FORWARD:
            handover(level).wait_send()
            pltpu.make_async_copy(received(level), received(level), send_sem.at[level - 1]).wait()
        else:
            pltpu.make_async_copy(lands[level - 1], lands[level - 1], send_sem.at[level - 1]).wait()
    mine = pl.ds(pl.multiple_of(z * PIECE, PIECE), PIECE)
    for half in range(2):
        short, index = hop(1 - half, 1, 0, 2)
        short.wait_recv()
        partial[mine, columns_of(half, 0)] += ring[index].astype(F32)
    for copy in hops[-4:-2]:
        copy.wait_send()
    for half in range(2):
        long, index = hop(half, 0, 0, 3)
        long.wait_recv()
        columns = columns_of(half, 0)
        out_ref[:, columns] = (partial[mine, columns] + ring[index].astype(F32)).astype(BF16)
    for copy in hops[-2:]:
        copy.wait_send()


def shards(tokens, w_query, w_key, w_value, w_out):
    message = [(2 * (ROWS >> level), WIDTH) for level in range(1, LEVELS + 1)]
    return pl.pallas_call(
        kernel,
        out_shape=jax.ShapeDtypeStruct((PIECE, MODEL), BF16),
        in_specs=[pl.BlockSpec(memory_space=pl.ANY)] * 5,
        out_specs=pl.BlockSpec(memory_space=pltpu.VMEM),
        scratch_shapes=[
            pltpu.VMEM((ROWS, MODEL), BF16),
            pltpu.VMEM((MODEL, WIDTH), BF16),
            pltpu.VMEM((MODEL, WIDTH), BF16),
            pltpu.VMEM((MODEL, WIDTH), BF16),
            pltpu.VMEM((WIDTH, MODEL), BF16),
            *[pltpu.VMEM(shape, BF16) for shape in message],
            *[pltpu.VMEM((1 << i, *shape), BF16) for i, shape in enumerate(message)],
            pltpu.VMEM((LEVELS, 2, ROWS, 2 * HEAD_DIM), BF16),
            pltpu.VMEM((2, ROWS, HEAD_DIM), F32),
            pltpu.VMEM((2, ROWS, HEAD_DIM), F32),
            pltpu.VMEM((2, ROWS, HEAD_DIM), F32),
            pltpu.VMEM((2, FAR, 2 * HEAD_DIM), BF16),
            pltpu.VMEM((2, FAR, HEAD_DIM), BF16),
            pltpu.VMEM((ROWS, MODEL), F32),
            pltpu.VMEM((14 * PARTS, PIECE, COLS), BF16),
            pltpu.VMEM((14 * PARTS, PIECE, COLS), BF16),
            pltpu.SemaphoreType.DMA((3 * CHUNKS + 2,)),
            pltpu.SemaphoreType.DMA((LEVELS,)),
            pltpu.SemaphoreType.DMA((LEVELS,)),
            pltpu.SemaphoreType.DMA((LEVELS,)),
            pltpu.SemaphoreType.DMA((LEVELS,)),
            pltpu.SemaphoreType.DMA((14 * PARTS,)),
            pltpu.SemaphoreType.DMA((14 * PARTS,)),
        ],
        compiler_params=pltpu.CompilerParams(
            collective_id=0, has_side_effects=True, vmem_limit_bytes=VMEM_BYTES
        ),
    )(tokens, w_query, w_key, w_value, w_out)


def solution(mesh):
    placed = (P("seq", None), P(None, "head"), P(None, "head"), P(None, "head"), P("head", None))
    return jax.shard_map(
        shards, mesh=mesh, in_specs=placed, out_specs=P(("seq", "head"), None), check_vma=False
    )
```
